32 devices in a mesh: groups: 2 (over y), variant: 16 (over z, x, core), tensor: 1.
Axes of the slice: x: 2, y: 2, z: 4, core: 2. Of those that a mesh axis runs over, the one named last changes fastest.
Arguments:
- hidden: bfloat16 [512, 8192], P(('groups', 'variant'), 'tensor'), parts along dimension 0, may hold values from -6 to 6
- norm_gain: bfloat16 [8192], P('tensor'), may hold values from 0.5 to 1.5
- base_weight: bfloat16 [8192, 512], P('tensor'), may hold values from -0.0625 to 0.0625
- delta_codes: bfloat16 [1, 32, 1024, 512], P('tensor', ('groups', 'variant')), parts along dimension 1, may hold values from 0 to 15
- delta_scales: float32 [1, 32, 8, 512], P('tensor', ('groups', 'variant')), parts along dimension 1, may hold values from 0.0003 to 0.003
- delta_zeros: float32 [1, 32, 8, 512], P('tensor', ('groups', 'variant')), parts along dimension 1, may hold values from 6 to 9
- variant_ids: int32 [512, 1], P(('groups', 'variant')), parts along dimension 0, may hold values from 0 to 1; in each aligned block of 16 rows (0 to 15, 16 to 31, ...) at most 16 rows name the same one
- positions: int32 [512], P(('groups', 'variant')), parts along dimension 0, may hold values from 0 to 8191
Outputs:
- keys: bfloat16 [512, 512], P(('groups', 'variant'), 'tensor'), parts along dimension 0
The draws below stay inside these ranges and needn't reach their ends.
There are 2 independent parts, one for each index of `groups`. The reference program is written for one: setup_inputs(seed, part) draws one part's arguments, and reference() takes and returns one part's arrays. A program takes and returns all parts, laid end to end along the dimension named above; an argument that names none is the same for every part. Nothing has to cross between parts.
Inputs may be any that keep to these rules, and one draw needn't show every extreme that they name: `variant_ids`: in each aligned block of 16 rows (the rows of one device along `variant`) no variant is named by more than 16 rows, and in some block one variant is named by exactly 16 rows; every variant is named by some row.
All inputs are finite; a program needn't handle non-finite values.
Results may differ from the reference program's by a relative error of at most 0.0075.
Values may be sent and summed in bfloat16 or wider, within the bound.
No kernel may reach another device: no remote copies, remote signals or barrier semaphores. Data moves between devices by JAX's collectives and lax.ppermute only.
A program may use at most 64 MiB of HBM per device.

```python
import math
import jax
import jax.numpy as jnp
import numpy as np
from jax import lax

D = 8192
HEAD = 128
GROUP = 128
OWNERS = 8
R_DEV = 16
KC = 512
SLICE = 1024
VARIANTS = 2
CAP = 16
ROWS = 256
N_TENSOR = 1


def place_ends(values, rng, smallest, largest):
    index_at = [jax.random.randint(jax.random.fold_in(rng, axis), (), 0, length) for axis, length in enumerate(values.shape)]
    main_axis = values.shape.index(max(values.shape))
    neighbour = index_at[:main_axis] + [(index_at[main_axis] + 1) % values.shape[main_axis]] + index_at[main_axis + 1:]
    return values.at[tuple(index_at)].set(smallest).at[tuple(neighbour)].set(largest)


def block_scale(own_key, dims, shards, low, largest):
    gain, own = 1.0, jax.random.fold_in(own_key, 6)
    for dim, parts in shards:
        draws = jnp.exp(jax.random.uniform(jax.random.fold_in(own, dim), (parts,), jnp.float32, low / len(shards), largest / len(shards)))
        gain = gain * jnp.repeat(draws, dims[dim] // parts).reshape([-1 if axis == dim else 1 for axis in range(len(dims))])
    return gain


def routed_block(own_key, own, number, rows, number_of, top, reach, skew):
    ranking = jax.random.permutation(own_key, number_of)
    heavy_load, ordinary = portions_of(number_of, rows * top, reach, skew, True), portions_of(number_of, rows * top, reach, skew, False)
    places = jnp.arange(number_of)

    def named(lengths, offset_by):
        used = int((lengths > 0).sum())
        fixed = max(1, used // 4)
        passed = fixed + (places - fixed + offset_by * (used - fixed)) % max(1, number_of - fixed)
        return jnp.zeros((number_of,), jnp.int32).at[ranking[jnp.where(places < fixed, places, passed)]].set(jnp.asarray(lengths, jnp.int32))

    lengths = jnp.where(number % 4 == 0, named(heavy_load, number // 4), named(ordinary, number - number // 4 - 1))
    mixed = jax.random.permutation(jax.random.fold_in(own, 3), number_of)
    giver, receiver = mixed[0:number_of // 2 * 2:2], mixed[1:number_of // 2 * 2:2]
    room = jnp.minimum(lengths[giver] - 1, reach - lengths[receiver]) // 2
    room = jnp.where((giver == ranking[0]) | (receiver == ranking[0]) | (lengths[receiver] == 0), 0, jnp.maximum(room, 0))
    passed = jax.random.randint(jax.random.fold_in(own, 4), (number_of // 2,), 0, 1 << 20) % (room + 1)
    lengths = lengths.at[giver].add(-passed).at[receiver].add(passed)
    items = jnp.searchsorted(jnp.cumsum(lengths), jnp.arange(rows * top), side="right").astype(jnp.int32)
    table = items.reshape(top, rows).T
    table = table[jax.random.permutation(jax.random.fold_in(own, 1), rows)]
    offset_by = jax.random.randint(jax.random.fold_in(own, 2), (rows, 1), 0, top)
    return jnp.take_along_axis(table, (jnp.arange(top)[None, :] + offset_by) % top, axis=1)


def portions_of(number_of, total, most, skew, full):
    loads = [(1 << 20) // math.isqrt(rank ** skew) + 1 for rank in range(1, number_of + 1)]
    largest = most if full else min(most, max(-(-total // number_of), total * loads[0] // sum(loads)))
    least = 1 if total - largest >= number_of - 1 else 0
    given, spare = [largest] + [least] * (number_of - 1), total - largest - least * (number_of - 1)
    while spare > 0:
        movable = [i for i in range(1, number_of) if given[i] < largest] or [i for i in range(1, number_of) if given[i] < most]
        pool, budget = sum([loads[i] for i in movable]), spare
        for i in movable:
            extra = min(most - given[i], max(1, budget * loads[i] // pool), spare)
            given[i] = given[i] + extra
            spare = spare - extra
    return np.array(given)


def normal_values(stream_key, dims, scale, reach, split=(), kind=jnp.bfloat16):
    result = jax.random.normal(stream_key, dims, jnp.float32) * scale
    if len(split) > 0:
        result = block_scale(stream_key, dims, split, -0.22, 0.18) * result
    return jnp.clip(result, min=-reach, max=reach).astype(kind)


def setup_inputs(seed: int = 0, part: int = 0) -> dict:
    key_of = jax.random.split(jax.random.key(seed), 9)
    own_keys = jax.random.split(jax.random.fold_in(key_of[8], part), 9)
    hidden = normal_values(own_keys[0], (ROWS, D), 1.0, 6.0, ((0, 16),))
    norm_gain = jnp.clip(1.0 + 0.1 * jax.random.normal(key_of[1], (D,), jnp.float32), 0.5, 1.5).astype(jnp.bfloat16)
    base_weight = normal_values(key_of[2], (D, KC), D ** -0.5, 0.0625)
    delta_codes = jnp.clip(15.0 * jax.random.uniform(own_keys[3], (N_TENSOR, VARIANTS * OWNERS, SLICE, KC), jnp.float32) ** block_scale(own_keys[3], (N_TENSOR, VARIANTS * OWNERS, SLICE, KC), ((1, 16),), -0.2, 0.2), 0.0, 15.0).astype(jnp.bfloat16)
    delta_scales = jnp.clip(jnp.exp(math.log(0.003) - 2.3025851 * jax.random.uniform(own_keys[4], (N_TENSOR, VARIANTS * OWNERS, SLICE // GROUP, KC), jnp.float32) ** block_scale(own_keys[4], (N_TENSOR, VARIANTS * OWNERS, SLICE // GROUP, KC), ((1, 16),), -0.2, 0.2)), 0.0003, 0.003)
    delta_zeros = jnp.clip(6.0 + 3.0 * jax.random.uniform(own_keys[5], (N_TENSOR, VARIANTS * OWNERS, SLICE // GROUP, KC), jnp.float32) ** block_scale(own_keys[5], (N_TENSOR, VARIANTS * OWNERS, SLICE // GROUP, KC), ((1, 16),), -0.2, 0.2), 6.0, 9.0)
    variant_ids_keys = jax.random.split(jax.random.fold_in(own_keys[6], 1), ROWS // R_DEV)
    variant_ids_turns = jax.random.permutation(jax.random.fold_in(own_keys[6], 3), ROWS // R_DEV)
    variant_ids = jax.vmap(lambda own, number: routed_block(jax.random.fold_in(own_keys[6], 2), own, number, R_DEV, VARIANTS, 1, CAP, 2))(variant_ids_keys, variant_ids_turns).reshape((ROWS, 1))
    positions = place_ends(jax.random.randint(own_keys[7], (ROWS,), 0, 8192), jax.random.fold_in(own_keys[7], 1), 0, 8191).astype(jnp.int32)
    return dict(hidden=hidden, norm_gain=norm_gain, base_weight=base_weight, delta_codes=delta_codes, delta_scales=delta_scales, delta_zeros=delta_zeros, variant_ids=variant_ids, positions=positions)


rope_theta = 500000.0
epsilon = 1e-05

def rotate_keys(projected, position):
    row_count = projected.shape[0]
    head_count = projected.shape[1] // HEAD
    half_size = HEAD // 2
    per_head = projected.reshape(row_count, head_count, HEAD)
    frequency = rope_theta ** (-(jnp.arange(half_size, dtype=jnp.float32) * 2.0 / HEAD))
    angles = position.astype(jnp.float32)[:, None] * frequency[None, :]
    cosine = jnp.cos(angles)[:, None, :]
    sine = jnp.sin(angles)[:, None, :]
    first = per_head[:, :, :half_size]
    second = per_head[:, :, half_size:]
    turned = jnp.concatenate([first * cosine - second * sine, second * cosine + first * sine], axis=2)
    return turned.reshape(row_count, head_count * HEAD).astype(jnp.bfloat16)

def dequantize(code_block, scale_block, zero_block):
    group_count = scale_block.shape[-2]
    leading_dims = code_block.shape[:-2]
    slice_rows = code_block.shape[-2]
    column_count = code_block.shape[-1]
    grouped = code_block.astype(jnp.float32).reshape(leading_dims + (group_count, slice_rows // group_count, column_count))
    values = (grouped - zero_block[..., :, None, :]) * scale_block[..., :, None, :]
    return values.reshape(leading_dims + (slice_rows, column_count))

def reference(hidden, norm_gain, base_weight, delta_codes, delta_scales, delta_zeros, variant_ids, positions):
    floats = hidden.astype(jnp.float32)
    mean_square = lax.optimization_barrier(jnp.sum(floats * floats, axis=1)) / D
    normed = (floats * lax.rsqrt(mean_square + epsilon)[:, None] * norm_gain.astype(jnp.float32)[None, :]).astype(jnp.bfloat16)
    projected = jnp.dot(normed, base_weight, preferred_element_type=jnp.float32)
    chosen = variant_ids[:, 0]

    def add_variant(carry, variant):
        start = (variant * OWNERS).astype(jnp.int32)
        code_block = lax.dynamic_slice_in_dim(delta_codes, start, OWNERS, 1)
        scale_block = lax.dynamic_slice_in_dim(delta_scales, start, OWNERS, 1)
        zero_block = lax.dynamic_slice_in_dim(delta_zeros, start, OWNERS, 1)
        delta_weight = dequantize(code_block, scale_block, zero_block).reshape(D, -1).astype(jnp.bfloat16)
        masked = jnp.where((chosen == variant)[:, None], normed, jnp.zeros_like(normed))
        return (carry + jnp.dot(masked, delta_weight, preferred_element_type=jnp.float32), None)
    delta_sum, _ = lax.scan(add_variant, jnp.zeros(projected.shape, jnp.float32), jnp.arange(VARIANTS, dtype=jnp.int32))
    return rotate_keys(projected + delta_sum, positions)
```

```python
import functools

import jax
import jax.numpy as jnp
from jax import lax
from jax.experimental import pallas as pl
from jax.experimental.pallas import tpu as pltpu
from jax.sharding import PartitionSpec as P

HEAD = 128
OWNERS = 8


rope_theta = 500000.0
epsilon = 1e-05


def rotate_keys(projected, position):
    row_count = projected.shape[0]
    head_count = projected.shape[1] // HEAD
    half_size = HEAD // 2
    per_head = projected.reshape(row_count, head_count, HEAD)
    frequency = rope_theta ** (-(jnp.arange(half_size, dtype=jnp.float32) * 2.0 / HEAD))
    angles = position.astype(jnp.float32)[:, None] * frequency[None, :]
    cosine = jnp.cos(angles)[:, None, :]
    sine = jnp.sin(angles)[:, None, :]
    first = per_head[:, :, :half_size]
    second = per_head[:, :, half_size:]
    turned = jnp.concatenate(
        [first * cosine - second * sine, second * cosine + first * sine], axis=2
    )
    return turned.reshape(row_count, head_count * HEAD).astype(jnp.bfloat16)


def dequantize(code_block, scale_block, zero_block):
    group_count = scale_block.shape[-2]
    leading_dims = code_block.shape[:-2]
    slice_rows = code_block.shape[-2]
    column_count = code_block.shape[-1]
    grouped = code_block.astype(jnp.float32).reshape(
        leading_dims + (group_count, slice_rows // group_count, column_count)
    )
    values = (grouped - zero_block[..., :, None, :]) * scale_block[..., :, None, :]
    return values.reshape(leading_dims + (slice_rows, column_count))


def general(
    hidden, norm_gain, base_weight, delta_codes, delta_scales, delta_zeros, variant_ids, positions
):
    row_count, half_width = hidden.shape
    device_count = lax.axis_size("variant")
    variant_count = device_count // OWNERS
    capacity = min(row_count, max(2, 2 * row_count // variant_count))
    slice_rows = delta_codes.shape[2]
    column_count = base_weight.shape[1]
    floats = hidden.astype(jnp.float32)
    local_squares = jnp.sum(floats * floats, axis=1)
    all_squares = lax.psum(local_squares, "tensor")
    full_width = half_width * lax.axis_size("tensor")
    normed = (
        floats
        * lax.rsqrt(all_squares / full_width + epsilon)[:, None]
        * norm_gain.astype(jnp.float32)[None, :]
    ).astype(jnp.bfloat16)
    chosen = variant_ids[:, 0]
    labels = jnp.arange(variant_count, dtype=jnp.int32)
    member = (chosen[:, None] == labels[None, :]).astype(jnp.int32)
    earlier = jnp.cumsum(member, axis=0) - member
    ranking = jnp.sum(earlier * member, axis=1)
    target_slot = chosen * capacity + ranking
    slot_labels = jnp.arange(variant_count * capacity, dtype=jnp.int32)
    placing = slot_labels[:, None] == target_slot[None, :]
    place_send = placing.astype(jnp.bfloat16).reshape(variant_count, capacity, row_count)
    place_back = placing.astype(jnp.float32)
    feature_pieces = normed.reshape(row_count, OWNERS, slice_rows)
    outgoing = jnp.einsum(
        "vcr,rjs->vjcs", place_send, feature_pieces, preferred_element_type=jnp.float32
    )
    outgoing = outgoing.astype(jnp.bfloat16).reshape(device_count, capacity, slice_rows)
    local_delta = dequantize(delta_codes[0, 0], delta_scales[0, 0], delta_zeros[0, 0]).astype(
        jnp.bfloat16
    )
    products = jnp.einsum(
        "acs,sk->ack",
        lax.all_to_all(outgoing, "variant", split_axis=0, concat_axis=0, tiled=True),
        local_delta,
        preferred_element_type=jnp.float32,
    )
    base_part = jnp.dot(normed, base_weight, preferred_element_type=jnp.float32)
    returned = lax.all_to_all(products, "variant", split_axis=0, concat_axis=0, tiled=True)
    summed = jnp.sum(returned.reshape(variant_count, OWNERS, capacity, column_count), axis=1)
    summed = summed.reshape(variant_count * capacity, column_count)
    delta_rows = jnp.einsum("sr,sk->rk", place_back, summed, precision=lax.Precision.HIGHEST)
    combined = lax.psum_scatter(base_part + delta_rows, "tensor", scatter_dimension=1, tiled=True)
    return rotate_keys(combined, positions)


def prepare_kernel(pieces, ids_ref, hidden_ref, gain_ref, out_ref):
    floats = hidden_ref[...].astype(jnp.float32)
    row_count, width = floats.shape
    mean_square = jnp.sum(floats * floats, axis=1, keepdims=True) / width
    normed = floats * lax.rsqrt(mean_square + epsilon) * gain_ref[...].astype(jnp.float32)
    square = (row_count, row_count)
    diagonal = lax.broadcasted_iota(jnp.int32, square, 0) == lax.broadcasted_iota(jnp.int32, square, 1)
    ids = jnp.sum(jnp.where(diagonal, ids_ref[...], 0), axis=1, keepdims=True)
    piece_width = width // pieces
    for variant in range(out_ref.shape[0] // pieces):
        kept = jnp.where(ids == variant, normed, 0.0).astype(jnp.bfloat16)
        for piece in range(pieces):
            out_ref[variant * pieces + piece] = kept[:, piece * piece_width : (piece + 1) * piece_width]


def weight_kernel(
    core_ref, own_codes, other_codes, own_groups, other_groups, base, out_ref, codes, groups, arrived
):
    slice_rows = codes.shape[1]
    core = core_ref[0]
    copies = [
        pltpu.make_async_copy(own_groups, groups.at[core], arrived.at[0]),
        pltpu.make_async_copy(other_groups, groups.at[1 - core], arrived.at[1]),
        pltpu.make_async_copy(own_codes, codes.at[core], arrived.at[2]),
        pltpu.make_async_copy(other_codes, codes.at[1 - core], arrived.at[3]),
    ]
    for copy in copies:
        copy.start()
    for copy in copies:
        copy.wait()
    group_count = groups.shape[1] // 2
    size = slice_rows // group_count
    for half in range(2):
        for group in range(group_count):
            rows = slice(group * size, (group + 1) * size)
            scale = groups[half, group : group + 1]
            zero = groups[half, group_count + group : group_count + group + 1]
            delta = (codes[half, rows].astype(jnp.float32) - zero) * scale
            rows = slice(half * slice_rows + group * size, half * slice_rows + (group + 1) * size)
            out_ref[rows] = (base[rows].astype(jnp.float32) + delta).astype(jnp.bfloat16)


def product_kernel(rows_ref, weight_ref, out_ref):
    count, size, width = rows_ref.shape
    rows = rows_ref[...].reshape(count * size, width)
    total = jnp.dot(rows, weight_ref[...], preferred_element_type=jnp.float32)
    out_ref[...] = total.reshape(out_ref.shape).astype(out_ref.dtype)


def finish_kernel(parts_ref, cosine_ref, sine_ref, out_ref):
    total = jnp.sum(parts_ref[...].astype(jnp.float32), axis=0)
    for head in range(total.shape[1] // HEAD):
        columns = slice(head * HEAD, (head + 1) * HEAD)
        block = total[:, columns]
        swapped = pltpu.roll(block, HEAD // 2, 1)
        out_ref[:, columns] = (block * cosine_ref[...] + swapped * sine_ref[...]).astype(out_ref.dtype)


def turn_factors(position):
    half_size = HEAD // 2
    frequency = rope_theta ** (-(jnp.arange(half_size, dtype=jnp.float32) * 2.0 / HEAD))
    angles = position.astype(jnp.float32)[:, None] * frequency[None, :]
    cosine, sine = jnp.cos(angles), jnp.sin(angles)
    return jnp.concatenate([cosine, cosine], axis=1), jnp.concatenate([-sine, sine], axis=1)


VMEM = pl.BlockSpec(memory_space=pltpu.VMEM)
SMEM = pl.BlockSpec(memory_space=pltpu.SMEM)
HBM = pl.BlockSpec(memory_space=pltpu.HBM)


def paired(
    hidden, norm_gain, base_weight, delta_codes, delta_scales, delta_zeros, variant_ids, positions
):
    row_count, width = hidden.shape
    device_count = lax.axis_size("variant")
    variant_count = device_count // OWNERS
    pieces = OWNERS // 2
    slice_rows, column_count = delta_codes.shape[2:]
    place = lax.axis_index("variant")
    parity = [list(range(first, device_count, 2)) for first in range(2)]
    swap = [(index, index ^ 1) for index in range(device_count)]

    own_codes = delta_codes[0, 0]
    own_groups = jnp.concatenate([delta_scales[0, 0], delta_zeros[0, 0]], axis=0)
    other_codes = lax.ppermute(own_codes, "variant", swap)
    other_groups = lax.ppermute(own_groups, "variant", swap)
    outgoing = pl.pallas_call(
        functools.partial(prepare_kernel, pieces),
        out_shape=jax.ShapeDtypeStruct((variant_count * pieces, row_count, width // pieces), jnp.bfloat16),
        in_specs=[VMEM] * 3,
        out_specs=VMEM,
        compiler_params=pltpu.CompilerParams(vmem_limit_bytes=16 << 20),
        name="prepare",
    )(variant_ids.T, hidden, norm_gain[None, :])
    both_rows = 2 * slice_rows
    weight = pl.pallas_call(
        weight_kernel,
        out_shape=jax.ShapeDtypeStruct((both_rows, column_count), jnp.bfloat16),
        in_specs=[SMEM] + [pl.BlockSpec(memory_space=pl.ANY)] * 4 + [VMEM],
        out_specs=VMEM,
        scratch_shapes=[
            pltpu.VMEM((2, slice_rows, column_count), jnp.bfloat16),
            pltpu.VMEM((2,) + own_groups.shape, jnp.float32),
            pltpu.SemaphoreType.DMA((4,)),
        ],
        compiler_params=pltpu.CompilerParams(vmem_limit_bytes=16 << 20),
        cost_estimate=pl.CostEstimate(
            flops=4 * both_rows * column_count, bytes_accessed=6 * both_rows * column_count, transcendentals=0
        ),
        name="weight",
    )(
        lax.rem(place, 2)[None],
        own_codes,
        other_codes,
        own_groups,
        other_groups,
        lax.dynamic_slice_in_dim(base_weight, lax.div(lax.rem(place, OWNERS), 2) * both_rows, both_rows, 0),
    )
    incoming = lax.all_to_all(
        outgoing, "variant", split_axis=0, concat_axis=0, tiled=True, axis_index_groups=parity
    )
    products = pl.pallas_call(
        product_kernel,
        out_shape=jax.ShapeDtypeStruct((device_count // 2, row_count, column_count), jnp.bfloat16),
        in_specs=[VMEM, VMEM],
        out_specs=VMEM,
        compiler_params=pltpu.CompilerParams(vmem_limit_bytes=16 << 20),
        name="product",
    )(incoming, weight)
    returned = lax.all_to_all(
        products, "variant", split_axis=0, concat_axis=0, tiled=True, axis_index_groups=parity
    )
    cosine, sine = turn_factors(positions)
    return pl.pallas_call(
        finish_kernel,
        out_shape=jax.ShapeDtypeStruct((row_count, column_count), jnp.bfloat16),
        in_specs=[VMEM] * 3,
        out_specs=VMEM,
        compiler_params=pltpu.CompilerParams(vmem_limit_bytes=8 << 20),
        name="finish",
    )(returned, cosine, sine)


def solution(mesh):
    devices = mesh.shape["variant"]
    small = mesh.shape["tensor"] == 1 and devices == 2 * OWNERS
    per_device = paired if small else general
    in_specs = (
        P(("groups", "variant"), "tensor"),
        P("tensor"),
        P("tensor", None),
        P("tensor", ("groups", "variant"), None, None),
        P("tensor", ("groups", "variant"), None, None),
        P("tensor", ("groups", "variant"), None, None),
        P(("groups", "variant"), None),
        P(("groups", "variant")),
    )
    out_specs = P(("groups", "variant"), "tensor")
    return jax.shard_map(
        per_device, mesh=mesh, in_specs=in_specs, out_specs=out_specs, check_vma=False
    )
```

```python
import functools

import jax
import jax.numpy as jnp
from jax import lax
from jax.experimental import pallas as pl
from jax.experimental.pallas import tpu as pltpu
from jax.sharding import PartitionSpec as P

HEAD = 128
OWNERS = 8


rope_theta = 500000.0
epsilon = 1e-05


def rotate_keys(projected, position):
    row_count = projected.shape[0]
    head_count = projected.shape[1] // HEAD
    half_size = HEAD // 2
    per_head = projected.reshape(row_count, head_count, HEAD)
    frequency = rope_theta ** (-(jnp.arange(half_size, dtype=jnp.float32) * 2.0 / HEAD))
    angles = position.astype(jnp.float32)[:, None] * frequency[None, :]
    cosine = jnp.cos(angles)[:, None, :]
    sine = jnp.sin(angles)[:, None, :]
    first = per_head[:, :, :half_size]
    second = per_head[:, :, half_size:]
    turned = jnp.concatenate(
        [first * cosine - second * sine, second * cosine + first * sine], axis=2
    )
    return turned.reshape(row_count, head_count * HEAD).astype(jnp.bfloat16)


def dequantize(code_block, scale_block, zero_block):
    group_count = scale_block.shape[-2]
    leading_dims = code_block.shape[:-2]
    slice_rows = code_block.shape[-2]
    column_count = code_block.shape[-1]
    grouped = code_block.astype(jnp.float32).reshape(
        leading_dims + (group_count, slice_rows // group_count, column_count)
    )
    values = (grouped - zero_block[..., :, None, :]) * scale_block[..., :, None, :]
    return values.reshape(leading_dims + (slice_rows, column_count))


def general(
    hidden, norm_gain, base_weight, delta_codes, delta_scales, delta_zeros, variant_ids, positions
):
    row_count, half_width = hidden.shape
    device_count = lax.axis_size("variant")
    variant_count = device_count // OWNERS
    capacity = min(row_count, max(2, 2 * row_count // variant_count))
    slice_rows = delta_codes.shape[2]
    column_count = base_weight.shape[1]
    floats = hidden.astype(jnp.float32)
    local_squares = jnp.sum(floats * floats, axis=1)
    all_squares = lax.psum(local_squares, "tensor")
    full_width = half_width * lax.axis_size("tensor")
    normed = (
        floats
        * lax.rsqrt(all_squares / full_width + epsilon)[:, None]
        * norm_gain.astype(jnp.float32)[None, :]
    ).astype(jnp.bfloat16)
    chosen = variant_ids[:, 0]
    labels = jnp.arange(variant_count, dtype=jnp.int32)
    member = (chosen[:, None] == labels[None, :]).astype(jnp.int32)
    earlier = jnp.cumsum(member, axis=0) - member
    ranking = jnp.sum(earlier * member, axis=1)
    target_slot = chosen * capacity + ranking
    slot_labels = jnp.arange(variant_count * capacity, dtype=jnp.int32)
    placing = slot_labels[:, None] == target_slot[None, :]
    place_send = placing.astype(jnp.bfloat16).reshape(variant_count, capacity, row_count)
    place_back = placing.astype(jnp.float32)
    feature_pieces = normed.reshape(row_count, OWNERS, slice_rows)
    outgoing = jnp.einsum(
        "vcr,rjs->vjcs", place_send, feature_pieces, preferred_element_type=jnp.float32
    )
    outgoing = outgoing.astype(jnp.bfloat16).reshape(device_count, capacity, slice_rows)
    local_delta = dequantize(delta_codes[0, 0], delta_scales[0, 0], delta_zeros[0, 0]).astype(
        jnp.bfloat16
    )
    products = jnp.einsum(
        "acs,sk->ack",
        lax.all_to_all(outgoing, "variant", split_axis=0, concat_axis=0, tiled=True),
        local_delta,
        preferred_element_type=jnp.float32,
    )
    base_part = jnp.dot(normed, base_weight, preferred_element_type=jnp.float32)
    returned = lax.all_to_all(products, "variant", split_axis=0, concat_axis=0, tiled=True)
    summed = jnp.sum(returned.reshape(variant_count, OWNERS, capacity, column_count), axis=1)
    summed = summed.reshape(variant_count * capacity, column_count)
    delta_rows = jnp.einsum("sr,sk->rk", place_back, summed, precision=lax.Precision.HIGHEST)
    combined = lax.psum_scatter(base_part + delta_rows, "tensor", scatter_dimension=1, tiled=True)
    return rotate_keys(combined, positions)


def norm_kernel(rows_ref, gain_ref, out_ref, gains_ref):
    gains_ref[...] = gain_ref[...].astype(jnp.float32).reshape(gains_ref.shape)
    out_ref[...] = norm_rows(rows_ref[...], gains_ref[...])


def weight_kernel(
    core_ref, first_ref, own_codes, other_codes, own_groups, other_groups, base_ref, out_ref, codes, groups, base, arrived
):
    slice_rows = codes.shape[1]
    core = core_ref[0]
    start = pl.multiple_of(first_ref[0] * slice_rows, slice_rows)
    copies = [
        pltpu.make_async_copy(own_groups, groups.at[core], arrived.at[0]),
        pltpu.make_async_copy(other_groups, groups.at[1 - core], arrived.at[1]),
        pltpu.make_async_copy(own_codes, codes.at[core], arrived.at[2]),
        pltpu.make_async_copy(base_ref.at[pl.ds(start, 2 * slice_rows)], base, arrived.at[3]),
        pltpu.make_async_copy(other_codes, codes.at[1 - core], arrived.at[4]),
    ]
    for copy in copies:
        copy.start()
    for copy in copies:
        copy.wait()
    group_count = groups.shape[1] // 2
    size = slice_rows // group_count
    for half in range(2):
        for group in range(group_count):
            rows = slice(group * size, (group + 1) * size)
            scale = groups[half, group : group + 1]
            zero = groups[half, group_count + group : group_count + group + 1]
            delta = (codes[half, rows].astype(jnp.float32) - zero) * scale
            rows = slice(half * slice_rows + group * size, half * slice_rows + (group + 1) * size)
            out_ref[rows] = (base[rows].astype(jnp.float32) + delta).astype(jnp.bfloat16)


def norm_rows(rows, gain):
    floats = rows.astype(jnp.float32)
    mean_square = jnp.sum(floats * floats, axis=1, keepdims=True) / rows.shape[1]
    return (floats * lax.rsqrt(mean_square + epsilon) * gain).astype(jnp.bfloat16)


def pieces_kernel(first_ref, core_ref, own_ref, other_ref, gain_ref, *rest):
    outs, normed_ref = rest[:-1], rest[-1]
    row_count = own_ref.shape[0]
    core = core_ref[0]
    normed_ref[pl.ds(pl.multiple_of(core * row_count, row_count), row_count)] = own_ref[...]
    other_rows = pl.ds(pl.multiple_of((1 - core) * row_count, row_count), row_count)
    normed_ref[other_rows] = norm_rows(other_ref[...], gain_ref[...])
    for index, out_ref in enumerate(outs):
        piece_width = out_ref.shape[1]
        start = pl.multiple_of((first_ref[0] ^ index) * piece_width, piece_width)
        out_ref[...] = normed_ref[:, pl.ds(start, piece_width)]


def product_kernel(rows_ref, weight_ref, out_ref):
    out_ref[...] = jnp.dot(rows_ref[...], weight_ref[...], preferred_element_type=jnp.float32).astype(out_ref.dtype)


def sum_kernel(core_ref, far_a, far_b, near_a, near_b, kept_ref, sent_ref, total_ref):
    total_ref[0] = far_a[...].astype(jnp.float32) + far_b[...].astype(jnp.float32)
    total_ref[1] = near_a[...].astype(jnp.float32) + near_b[...].astype(jnp.float32)
    row_count = kept_ref.shape[1]
    core = core_ref[0]
    kept_ref[...] = total_ref[:, pl.ds(pl.multiple_of(core * row_count, row_count), row_count)]
    sent_ref[...] = total_ref[:, pl.ds(pl.multiple_of((1 - core) * row_count, row_count), row_count)]


def finish_kernel(variant_ref, ids_ref, kept_ref, received_ref, cosine_ref, sine_ref, out_ref):
    row_count, column_count = out_ref.shape
    square = (row_count, row_count)
    diagonal = lax.broadcasted_iota(jnp.int32, square, 0) == lax.broadcasted_iota(jnp.int32, square, 1)
    ids = jnp.sum(jnp.where(diagonal, ids_ref[...], 0), axis=1, keepdims=True)
    near = ids == variant_ref[0]
    total = jnp.where(near, kept_ref[1] + received_ref[1], kept_ref[0] + received_ref[0])
    for head in range(column_count // HEAD):
        columns = slice(head * HEAD, (head + 1) * HEAD)
        block = total[:, columns]
        swapped = pltpu.roll(block, HEAD // 2, 1)
        out_ref[:, columns] = (block * cosine_ref[...] + swapped * sine_ref[...]).astype(out_ref.dtype)


def turn_factors(position):
    half_size = HEAD // 2
    frequency = rope_theta ** (-(jnp.arange(half_size, dtype=jnp.float32) * 2.0 / HEAD))
    angles = position.astype(jnp.float32)[:, None] * frequency[None, :]
    cosine, sine = jnp.cos(angles), jnp.sin(angles)
    return jnp.concatenate([cosine, cosine], axis=1), jnp.concatenate([-sine, sine], axis=1)


VMEM = pl.BlockSpec(memory_space=pltpu.VMEM)
SMEM = pl.BlockSpec(memory_space=pltpu.SMEM)
ANY = pl.BlockSpec(memory_space=pl.ANY)


def paired(
    hidden, norm_gain, base_weight, delta_codes, delta_scales, delta_zeros, variant_ids, positions
):
    row_count, width = hidden.shape
    device_count = lax.axis_size("variant")
    pieces = OWNERS // 2
    slice_rows, column_count = delta_codes.shape[2:]
    place = lax.axis_index("variant")
    core = lax.rem(place, 2)
    piece = lax.div(lax.rem(place, OWNERS), 2)
    variant = lax.div(place, OWNERS)
    swap = [(index, index ^ 1) for index in range(device_count)]
    far = pieces
    steps = [(0, far, far + 2), (1, far + 1, far + 3), (1, 1, 3), (0, 0, 2)]
    routes = [
        [(index, index ^ (2 * distances[index % 2])) for index in range(device_count)] for _, *distances in steps
    ]

    slice_shape = (slice_rows, column_count)
    own_codes = delta_codes[0, 0]
    own_groups = jnp.concatenate([delta_scales[0, 0], delta_zeros[0, 0]], axis=0)
    other_hidden = lax.ppermute(hidden, "variant", swap)
    other_groups = lax.ppermute(own_groups, "variant", swap)
    normed, gains = pl.pallas_call(
        norm_kernel,
        out_shape=[jax.ShapeDtypeStruct((row_count, width), jnp.bfloat16), jax.ShapeDtypeStruct((1, width), jnp.float32)],
        in_specs=[VMEM] * 2,
        out_specs=[VMEM] * 2,
        compiler_params=pltpu.CompilerParams(vmem_limit_bytes=16 << 20),
        name="norm",
    )(hidden, norm_gain)
    other_hidden, other_groups, codes, normed = lax.optimization_barrier(
        (other_hidden, other_groups, own_codes, normed)
    )
    other_codes = lax.ppermute(codes, "variant", swap)
    first, second = pl.pallas_call(
        pieces_kernel,
        out_shape=[jax.ShapeDtypeStruct((2 * row_count, width // pieces), jnp.bfloat16)] * 2,
        in_specs=[SMEM, SMEM, VMEM, VMEM, VMEM],
        out_specs=[VMEM] * 2,
        scratch_shapes=[pltpu.VMEM((2 * row_count, width), jnp.bfloat16)],
        compiler_params=pltpu.CompilerParams(vmem_limit_bytes=16 << 20),
        name="pieces",
    )((piece ^ (2 * core))[None], core[None], normed, other_hidden, gains)
    weight = pl.pallas_call(
        weight_kernel,
        out_shape=jax.ShapeDtypeStruct((2 * slice_rows, column_count), jnp.bfloat16),
        in_specs=[SMEM, SMEM] + [ANY] * 5,
        out_specs=VMEM,
        scratch_shapes=[
            pltpu.VMEM((2,) + slice_shape, jnp.bfloat16),
            pltpu.VMEM((2,) + own_groups.shape, jnp.float32),
            pltpu.VMEM((2 * slice_rows, column_count), jnp.bfloat16),
            pltpu.SemaphoreType.DMA((5,)),
        ],
        compiler_params=pltpu.CompilerParams(vmem_limit_bytes=48 << 20),
        name="weight",
    )(core[None], (piece * 2)[None], own_codes, other_codes, own_groups, other_groups, base_weight)
    incoming = [lax.ppermute((first, second)[index], "variant", route) for (index, _, _), route in zip(steps, routes)]
    parts = [None] * len(steps)
    for step in (2, 3, 0, 1):
        product = pl.pallas_call(
            product_kernel,
            out_shape=jax.ShapeDtypeStruct((2 * row_count, column_count), jnp.bfloat16),
            in_specs=[VMEM, VMEM],
            out_specs=VMEM,
            compiler_params=pltpu.CompilerParams(vmem_limit_bytes=16 << 20),
            name="product",
        )(incoming[step], weight)
        parts[step] = lax.ppermute(product, "variant", routes[step])
    kept, sent = pl.pallas_call(
        sum_kernel,
        out_shape=[jax.ShapeDtypeStruct((2, row_count, column_count), jnp.float32)] * 2,
        in_specs=[SMEM] + [VMEM] * len(parts),
        out_specs=[VMEM] * 2,
        scratch_shapes=[pltpu.VMEM((2, 2 * row_count, column_count), jnp.float32)],
        compiler_params=pltpu.CompilerParams(vmem_limit_bytes=8 << 20),
        name="sum",
    )(core[None], *parts)
    received = lax.ppermute(sent, "variant", swap)
    cosine, sine = turn_factors(positions)
    return pl.pallas_call(
        finish_kernel,
        out_shape=jax.ShapeDtypeStruct((row_count, column_count), jnp.bfloat16),
        in_specs=[SMEM] + [VMEM] * 5,
        out_specs=VMEM,
        compiler_params=pltpu.CompilerParams(vmem_limit_bytes=8 << 20),
        name="finish",
    )(variant[None], variant_ids.T, kept, received, cosine, sine)


def solution(mesh):
    devices = mesh.shape["variant"]
    small = mesh.shape["tensor"] == 1 and devices == 2 * OWNERS
    per_device = paired if small else general
    in_specs = (
        P(("groups", "variant"), "tensor"),
        P("tensor"),
        P("tensor", None),
        P("tensor", ("groups", "variant"), None, None),
        P("tensor", ("groups", "variant"), None, None),
        P("tensor", ("groups", "variant"), None, None),
        P(("groups", "variant"), None),
        P(("groups", "variant")),
    )
    out_specs = P(("groups", "variant"), "tensor")
    return jax.shard_map(
        per_device, mesh=mesh, in_specs=in_specs, out_specs=out_specs, check_vma=False
    )
```

```python
import functools

import jax
import jax.numpy as jnp
from jax import lax
from jax.experimental import pallas as pl
from jax.experimental.pallas import tpu as pltpu
from jax.sharding import PartitionSpec as P

HEAD = 128
OWNERS = 8


rope_theta = 500000.0
epsilon = 1e-05


def rotate_keys(projected, position):
    row_count = projected.shape[0]
    head_count = projected.shape[1] // HEAD
    half_size = HEAD // 2
    per_head = projected.reshape(row_count, head_count, HEAD)
    frequency = rope_theta ** (-(jnp.arange(half_size, dtype=jnp.float32) * 2.0 / HEAD))
    angles = position.astype(jnp.float32)[:, None] * frequency[None, :]
    cosine = jnp.cos(angles)[:, None, :]
    sine = jnp.sin(angles)[:, None, :]
    first = per_head[:, :, :half_size]
    second = per_head[:, :, half_size:]
    turned = jnp.concatenate(
        [first * cosine - second * sine, second * cosine + first * sine], axis=2
    )
    return turned.reshape(row_count, head_count * HEAD).astype(jnp.bfloat16)


def dequantize(code_block, scale_block, zero_block):
    group_count = scale_block.shape[-2]
    leading_dims = code_block.shape[:-2]
    slice_rows = code_block.shape[-2]
    column_count = code_block.shape[-1]
    grouped = code_block.astype(jnp.float32).reshape(
        leading_dims + (group_count, slice_rows // group_count, column_count)
    )
    values = (grouped - zero_block[..., :, None, :]) * scale_block[..., :, None, :]
    return values.reshape(leading_dims + (slice_rows, column_count))


def general(
    hidden, norm_gain, base_weight, delta_codes, delta_scales, delta_zeros, variant_ids, positions
):
    row_count, half_width = hidden.shape
    device_count = lax.axis_size("variant")
    variant_count = device_count // OWNERS
    capacity = min(row_count, max(2, 2 * row_count // variant_count))
    slice_rows = delta_codes.shape[2]
    column_count = base_weight.shape[1]
    floats = hidden.astype(jnp.float32)
    local_squares = jnp.sum(floats * floats, axis=1)
    all_squares = lax.psum(local_squares, "tensor")
    full_width = half_width * lax.axis_size("tensor")
    normed = (
        floats
        * lax.rsqrt(all_squares / full_width + epsilon)[:, None]
        * norm_gain.astype(jnp.float32)[None, :]
    ).astype(jnp.bfloat16)
    chosen = variant_ids[:, 0]
    labels = jnp.arange(variant_count, dtype=jnp.int32)
    member = (chosen[:, None] == labels[None, :]).astype(jnp.int32)
    earlier = jnp.cumsum(member, axis=0) - member
    ranking = jnp.sum(earlier * member, axis=1)
    target_slot = chosen * capacity + ranking
    slot_labels = jnp.arange(variant_count * capacity, dtype=jnp.int32)
    placing = slot_labels[:, None] == target_slot[None, :]
    place_send = placing.astype(jnp.bfloat16).reshape(variant_count, capacity, row_count)
    place_back = placing.astype(jnp.float32)
    feature_pieces = normed.reshape(row_count, OWNERS, slice_rows)
    outgoing = jnp.einsum(
        "vcr,rjs->vjcs", place_send, feature_pieces, preferred_element_type=jnp.float32
    )
    outgoing = outgoing.astype(jnp.bfloat16).reshape(device_count, capacity, slice_rows)
    local_delta = dequantize(delta_codes[0, 0], delta_scales[0, 0], delta_zeros[0, 0]).astype(
        jnp.bfloat16
    )
    products = jnp.einsum(
        "acs,sk->ack",
        lax.all_to_all(outgoing, "variant", split_axis=0, concat_axis=0, tiled=True),
        local_delta,
        preferred_element_type=jnp.float32,
    )
    base_part = jnp.dot(normed, base_weight, preferred_element_type=jnp.float32)
    returned = lax.all_to_all(products, "variant", split_axis=0, concat_axis=0, tiled=True)
    summed = jnp.sum(returned.reshape(variant_count, OWNERS, capacity, column_count), axis=1)
    summed = summed.reshape(variant_count * capacity, column_count)
    delta_rows = jnp.einsum("sr,sk->rk", place_back, summed, precision=lax.Precision.HIGHEST)
    combined = lax.psum_scatter(base_part + delta_rows, "tensor", scatter_dimension=1, tiled=True)
    return rotate_keys(combined, positions)


def norm_kernel(rows_ref, gain_ref, out_ref, gains_ref, rows, gain, arrived):
    copies = [
        pltpu.make_async_copy(gain_ref, gain, arrived.at[0]),
        pltpu.make_async_copy(rows_ref, rows, arrived.at[1]),
    ]
    for copy in copies:
        copy.start()
    copies[0].wait()
    gains_ref[...] = gain[...].astype(jnp.float32).reshape(gains_ref.shape)
    copies[1].wait()
    out_ref[...] = norm_rows(rows[...], gains_ref[...])


def weight_kernel(
    core_ref,
    first_ref,
    own_codes,
    own_scales,
    own_zeros,
    base_ref,
    other_codes,
    other_scales,
    other_zeros,
    out_ref,
    codes,
    scales,
    zeros,
    base,
    arrived,
):
    slice_rows = codes.shape[0]
    core = core_ref[0]
    starts = [pl.multiple_of((1 - core) * slice_rows, slice_rows), pl.multiple_of(core * slice_rows, slice_rows)]
    first = first_ref[0] * slice_rows
    copies = [
        pltpu.make_async_copy(
            base_ref.at[pl.ds(pl.multiple_of(first + starts[0], slice_rows), slice_rows)], base.at[0], arrived.at[0]
        ),
        pltpu.make_async_copy(own_scales, scales, arrived.at[1]),
        pltpu.make_async_copy(own_zeros, zeros, arrived.at[2]),
        pltpu.make_async_copy(own_codes, codes, arrived.at[3]),
        pltpu.make_async_copy(
            base_ref.at[pl.ds(pl.multiple_of(first + starts[1], slice_rows), slice_rows)], base.at[1], arrived.at[4]
        ),
    ]
    for copy in copies:
        copy.start()
    group_count = scales.shape[0]
    size = slice_rows // group_count
    sources = [(other_codes, other_scales, other_zeros), (codes, scales, zeros)]
    for member, (member_codes, member_scales, member_zeros) in enumerate(sources):
        for copy in copies[1:] if member else copies[:1]:
            copy.wait()
        for group in range(group_count):
            rows = slice(group * size, (group + 1) * size)
            delta = member_codes[rows].astype(jnp.float32) - member_zeros[group : group + 1]
            delta = delta * member_scales[group : group + 1]
            target = pl.ds(pl.multiple_of(starts[member] + group * size, size), size)
            out_ref[target] = (base[member, rows].astype(jnp.float32) + delta).astype(jnp.bfloat16)


def norm_rows(rows, gain):
    floats = rows.astype(jnp.float32)
    mean_square = jnp.sum(floats * floats, axis=1, keepdims=True) / rows.shape[1]
    return (floats * lax.rsqrt(mean_square + epsilon) * gain).astype(jnp.bfloat16)


def pieces_kernel(first_ref, core_ref, own_ref, other_ref, gain_ref, *rest):
    outs, normed_ref = rest[:-1], rest[-1]
    row_count = own_ref.shape[0]
    core = core_ref[0]
    normed_ref[pl.ds(pl.multiple_of(core * row_count, row_count), row_count)] = own_ref[...]
    other_rows = pl.ds(pl.multiple_of((1 - core) * row_count, row_count), row_count)
    normed_ref[other_rows] = norm_rows(other_ref[...], gain_ref[...])
    for index, out_ref in enumerate(outs):
        piece_width = out_ref.shape[1]
        start = pl.multiple_of((first_ref[0] ^ index) * piece_width, piece_width)
        out_ref[...] = normed_ref[:, pl.ds(start, piece_width)]


def product_kernel(rows_ref, weight_ref, out_ref):
    out_ref[...] = jnp.dot(rows_ref[...], weight_ref[...], preferred_element_type=jnp.float32).astype(out_ref.dtype)


def sum_kernel(core_ref, far_a, near_a, far_b, near_b, kept_ref, sent_ref, total_ref):
    total_ref[0] = far_a[...].astype(jnp.float32) + far_b[...].astype(jnp.float32)
    total_ref[1] = near_a[...].astype(jnp.float32) + near_b[...].astype(jnp.float32)
    row_count = kept_ref.shape[1]
    core = core_ref[0]
    kept_ref[...] = total_ref[:, pl.ds(pl.multiple_of(core * row_count, row_count), row_count)]
    sent_ref[...] = total_ref[:, pl.ds(pl.multiple_of((1 - core) * row_count, row_count), row_count)]


def finish_kernel(variant_ref, ids_ref, kept_ref, received_ref, cosine_ref, sine_ref, out_ref):
    row_count, column_count = out_ref.shape
    square = (row_count, row_count)
    diagonal = lax.broadcasted_iota(jnp.int32, square, 0) == lax.broadcasted_iota(jnp.int32, square, 1)
    ids = jnp.sum(jnp.where(diagonal, ids_ref[...], 0), axis=1, keepdims=True)
    near = ids == variant_ref[0]
    total = jnp.where(near, kept_ref[1] + received_ref[1], kept_ref[0] + received_ref[0])
    for head in range(column_count // HEAD):
        columns = slice(head * HEAD, (head + 1) * HEAD)
        block = total[:, columns]
        swapped = pltpu.roll(block, HEAD // 2, 1)
        out_ref[:, columns] = (block * cosine_ref[...] + swapped * sine_ref[...]).astype(out_ref.dtype)


def turn_factors(position):
    half_size = HEAD // 2
    frequency = rope_theta ** (-(jnp.arange(half_size, dtype=jnp.float32) * 2.0 / HEAD))
    angles = position.astype(jnp.float32)[:, None] * frequency[None, :]
    cosine, sine = jnp.cos(angles), jnp.sin(angles)
    return jnp.concatenate([cosine, cosine], axis=1), jnp.concatenate([-sine, sine], axis=1)


VMEM = pl.BlockSpec(memory_space=pltpu.VMEM)
SMEM = pl.BlockSpec(memory_space=pltpu.SMEM)
ANY = pl.BlockSpec(memory_space=pl.ANY)


def in_hbm(array):
    return pltpu.with_memory_space_constraint(array, pltpu.HBM)


def paired(
    hidden, norm_gain, base_weight, delta_codes, delta_scales, delta_zeros, variant_ids, positions
):
    row_count, width = hidden.shape
    device_count = lax.axis_size("variant")
    pieces = OWNERS // 2
    slice_rows, column_count = delta_codes.shape[2:]
    place = lax.axis_index("variant")
    core = lax.rem(place, 2)
    piece = lax.div(lax.rem(place, OWNERS), 2)
    variant = lax.div(place, OWNERS)
    swap = [(index, index ^ 1) for index in range(device_count)]
    far = pieces
    steps = [(0, far, far + 2), (1, 1, 3), (1, far + 1, far + 3), (0, 0, 2)]
    routes = [
        [(index, index ^ (2 * distances[index % 2])) for index in range(device_count)] for _, *distances in steps
    ]

    slice_shape, group_shape = (slice_rows, column_count), delta_scales.shape[2:]
    own_codes, own_scales, own_zeros = delta_codes[0, 0], delta_scales[0, 0], delta_zeros[0, 0]
    other_hidden = lax.ppermute(hidden, "variant", swap)
    other_scales = lax.ppermute(own_scales, "variant", swap)
    other_zeros = lax.ppermute(own_zeros, "variant", swap)
    normed, gains = pl.pallas_call(
        norm_kernel,
        out_shape=[jax.ShapeDtypeStruct((row_count, width), jnp.bfloat16), jax.ShapeDtypeStruct((1, width), jnp.float32)],
        in_specs=[ANY] * 2,
        out_specs=[VMEM] * 2,
        scratch_shapes=[
            pltpu.VMEM((row_count, width), jnp.bfloat16),
            pltpu.VMEM((width,), jnp.bfloat16),
            pltpu.SemaphoreType.DMA((2,)),
        ],
        compiler_params=pltpu.CompilerParams(vmem_limit_bytes=16 << 20),
        name="norm",
    )(in_hbm(hidden), in_hbm(norm_gain))
    other_hidden, other_scales, other_zeros, codes, normed = lax.optimization_barrier(
        (other_hidden, other_scales, other_zeros, own_codes, normed)
    )
    other_codes = lax.ppermute(codes, "variant", swap)
    first, second = pl.pallas_call(
        pieces_kernel,
        out_shape=[jax.ShapeDtypeStruct((2 * row_count, width // pieces), jnp.bfloat16)] * 2,
        in_specs=[SMEM, SMEM, VMEM, VMEM, VMEM],
        out_specs=[VMEM] * 2,
        scratch_shapes=[pltpu.VMEM((2 * row_count, width), jnp.bfloat16)],
        compiler_params=pltpu.CompilerParams(vmem_limit_bytes=16 << 20),
        name="pieces",
    )((piece ^ (2 * core))[None], core[None], normed, other_hidden, gains)
    weight = pl.pallas_call(
        weight_kernel,
        out_shape=jax.ShapeDtypeStruct((2 * slice_rows, column_count), jnp.bfloat16),
        in_specs=[SMEM, SMEM] + [ANY] * 4 + [VMEM] * 3,
        out_specs=VMEM,
        scratch_shapes=[
            pltpu.VMEM(slice_shape, jnp.bfloat16),
            pltpu.VMEM(group_shape, jnp.float32),
            pltpu.VMEM(group_shape, jnp.float32),
            pltpu.VMEM((2,) + slice_shape, jnp.bfloat16),
            pltpu.SemaphoreType.DMA((5,)),
        ],
        compiler_params=pltpu.CompilerParams(vmem_limit_bytes=16 << 20),
        name="weight",
    )(
        core[None],
        (piece * 2)[None],
        in_hbm(own_codes),
        in_hbm(own_scales),
        in_hbm(own_zeros),
        in_hbm(base_weight),
        other_codes,
        other_scales,
        other_zeros,
    )
    weight, positions = lax.optimization_barrier((weight, positions))
    incoming = [lax.ppermute((first, second)[index], "variant", route) for (index, _, _), route in zip(steps, routes)]
    parts = [None] * len(steps)
    for step in range(len(steps)):
        product = pl.pallas_call(
            product_kernel,
            out_shape=jax.ShapeDtypeStruct((2 * row_count, column_count), jnp.bfloat16),
            in_specs=[VMEM, VMEM],
            out_specs=VMEM,
            compiler_params=pltpu.CompilerParams(vmem_limit_bytes=16 << 20),
            name="product",
        )(incoming[step], weight)
        parts[step] = lax.ppermute(product, "variant", routes[step])
    kept, sent = pl.pallas_call(
        sum_kernel,
        out_shape=[jax.ShapeDtypeStruct((2, row_count, column_count), jnp.float32)] * 2,
        in_specs=[SMEM] + [VMEM] * len(parts),
        out_specs=[VMEM] * 2,
        scratch_shapes=[pltpu.VMEM((2, 2 * row_count, column_count), jnp.float32)],
        compiler_params=pltpu.CompilerParams(vmem_limit_bytes=8 << 20),
        name="sum",
    )(core[None], *parts)
    received = lax.ppermute(sent, "variant", swap)
    cosine, sine = turn_factors(positions)
    return pl.pallas_call(
        finish_kernel,
        out_shape=jax.ShapeDtypeStruct((row_count, column_count), jnp.bfloat16),
        in_specs=[SMEM] + [VMEM] * 5,
        out_specs=VMEM,
        compiler_params=pltpu.CompilerParams(vmem_limit_bytes=8 << 20),
        name="finish",
    )(variant[None], variant_ids.T, kept, received, cosine, sine)


def solution(mesh):
    devices = mesh.shape["variant"]
    small = mesh.shape["tensor"] == 1 and devices == 2 * OWNERS
    per_device = paired if small else general
    in_specs = (
        P(("groups", "variant"), "tensor"),
        P("tensor"),
        P("tensor", None),
        P("tensor", ("groups", "variant"), None, None),
        P("tensor", ("groups", "variant"), None, None),
        P("tensor", ("groups", "variant"), None, None),
        P(("groups", "variant"), None),
        P(("groups", "variant")),
    )
    out_specs = P(("groups", "variant"), "tensor")
    return jax.shard_map(
        per_device, mesh=mesh, in_specs=in_specs, out_specs=out_specs, check_vma=False
    )
```

```python
import functools

import jax
import jax.numpy as jnp
from jax import lax
from jax.experimental import pallas as pl
from jax.experimental.pallas import tpu as pltpu
from jax.sharding import PartitionSpec as P

HEAD = 128
OWNERS = 8


rope_theta = 500000.0
epsilon = 1e-05


def rotate_keys(projected, position):
    row_count = projected.shape[0]
    head_count = projected.shape[1] // HEAD
    half_size = HEAD // 2
    per_head = projected.reshape(row_count, head_count, HEAD)
    frequency = rope_theta ** (-(jnp.arange(half_size, dtype=jnp.float32) * 2.0 / HEAD))
    angles = position.astype(jnp.float32)[:, None] * frequency[None, :]
    cosine = jnp.cos(angles)[:, None, :]
    sine = jnp.sin(angles)[:, None, :]
    first = per_head[:, :, :half_size]
    second = per_head[:, :, half_size:]
    turned = jnp.concatenate(
        [first * cosine - second * sine, second * cosine + first * sine], axis=2
    )
    return turned.reshape(row_count, head_count * HEAD).astype(jnp.bfloat16)


def dequantize(code_block, scale_block, zero_block):
    group_count = scale_block.shape[-2]
    leading_dims = code_block.shape[:-2]
    slice_rows = code_block.shape[-2]
    column_count = code_block.shape[-1]
    grouped = code_block.astype(jnp.float32).reshape(
        leading_dims + (group_count, slice_rows // group_count, column_count)
    )
    values = (grouped - zero_block[..., :, None, :]) * scale_block[..., :, None, :]
    return values.reshape(leading_dims + (slice_rows, column_count))


def general(
    hidden, norm_gain, base_weight, delta_codes, delta_scales, delta_zeros, variant_ids, positions
):
    row_count, half_width = hidden.shape
    device_count = lax.axis_size("variant")
    variant_count = device_count // OWNERS
    capacity = min(row_count, max(2, 2 * row_count // variant_count))
    slice_rows = delta_codes.shape[2]
    column_count = base_weight.shape[1]
    floats = hidden.astype(jnp.float32)
    local_squares = jnp.sum(floats * floats, axis=1)
    all_squares = lax.psum(local_squares, "tensor")
    full_width = half_width * lax.axis_size("tensor")
    normed = (
        floats
        * lax.rsqrt(all_squares / full_width + epsilon)[:, None]
        * norm_gain.astype(jnp.float32)[None, :]
    ).astype(jnp.bfloat16)
    chosen = variant_ids[:, 0]
    labels = jnp.arange(variant_count, dtype=jnp.int32)
    member = (chosen[:, None] == labels[None, :]).astype(jnp.int32)
    earlier = jnp.cumsum(member, axis=0) - member
    ranking = jnp.sum(earlier * member, axis=1)
    target_slot = chosen * capacity + ranking
    slot_labels = jnp.arange(variant_count * capacity, dtype=jnp.int32)
    placing = slot_labels[:, None] == target_slot[None, :]
    place_send = placing.astype(jnp.bfloat16).reshape(variant_count, capacity, row_count)
    place_back = placing.astype(jnp.float32)
    feature_pieces = normed.reshape(row_count, OWNERS, slice_rows)
    outgoing = jnp.einsum(
        "vcr,rjs->vjcs", place_send, feature_pieces, preferred_element_type=jnp.float32
    )
    outgoing = outgoing.astype(jnp.bfloat16).reshape(device_count, capacity, slice_rows)
    local_delta = dequantize(delta_codes[0, 0], delta_scales[0, 0], delta_zeros[0, 0]).astype(
        jnp.bfloat16
    )
    products = jnp.einsum(
        "acs,sk->ack",
        lax.all_to_all(outgoing, "variant", split_axis=0, concat_axis=0, tiled=True),
        local_delta,
        preferred_element_type=jnp.float32,
    )
    base_part = jnp.dot(normed, base_weight, preferred_element_type=jnp.float32)
    returned = lax.all_to_all(products, "variant", split_axis=0, concat_axis=0, tiled=True)
    summed = jnp.sum(returned.reshape(variant_count, OWNERS, capacity, column_count), axis=1)
    summed = summed.reshape(variant_count * capacity, column_count)
    delta_rows = jnp.einsum("sr,sk->rk", place_back, summed, precision=lax.Precision.HIGHEST)
    combined = lax.psum_scatter(base_part + delta_rows, "tensor", scatter_dimension=1, tiled=True)
    return rotate_keys(combined, positions)


def front_kernel(
    place_ref,
    hidden_ref,
    gain_ref,
    codes_ref,
    scales_ref,
    zeros_ref,
    base_ref,
    normed_ref,
    gains_ref,
    weight_ref,
    hidden,
    gain,
    codes,
    scales,
    zeros,
    base,
    arrived,
):
    slice_rows = codes.shape[0]
    half = slice_rows // 2
    start = place_ref[0] * slice_rows
    copies = [
        pltpu.make_async_copy(hidden_ref, hidden, arrived.at[0]),
        pltpu.make_async_copy(gain_ref, gain, arrived.at[1]),
        pltpu.make_async_copy(scales_ref, scales, arrived.at[2]),
        pltpu.make_async_copy(zeros_ref, zeros, arrived.at[3]),
    ]
    for part in range(2):
        rows = pl.ds(part * half, half)
        base_rows = pl.ds(pl.multiple_of(start + part * half, half), half)
        copies.append(pltpu.make_async_copy(codes_ref.at[rows], codes.at[rows], arrived.at[4 + 2 * part]))
        copies.append(pltpu.make_async_copy(base_ref.at[base_rows], base.at[rows], arrived.at[5 + 2 * part]))
    for copy in copies:
        copy.start()
    for copy in copies[:2]:
        copy.wait()
    gains_ref[...] = gain[...].astype(jnp.float32).reshape(gains_ref.shape)
    normed_ref[...] = norm_rows(hidden[...], gains_ref[...])
    for copy in copies[2:4]:
        copy.wait()
    group_count = scales.shape[0]
    size = slice_rows // group_count
    for group in range(group_count):
        if group == 0 or group == group_count // 2:
            part = 4 + 2 * (group > 0)
            for copy in copies[part : part + 2]:
                copy.wait()
        rows = slice(group * size, (group + 1) * size)
        delta = (codes[rows].astype(jnp.float32) - zeros[group : group + 1]) * scales[group : group + 1]
        weight_ref[rows] = (base[rows].astype(jnp.float32) + delta).astype(jnp.bfloat16)


def norm_rows(rows, gain):
    floats = rows.astype(jnp.float32)
    mean_square = jnp.sum(floats * floats, axis=1, keepdims=True) / rows.shape[1]
    return (floats * lax.rsqrt(mean_square + epsilon) * gain).astype(jnp.bfloat16)


def pieces_kernel(orders, piece_ref, core_ref, own_ref, other_ref, gain_ref, *rest):
    outs, normed_ref = rest[:-1], rest[-1]
    row_count = own_ref.shape[0]
    core = core_ref[0]
    normed_ref[pl.ds(pl.multiple_of(core * row_count, row_count), row_count)] = own_ref[...]
    other_rows = pl.ds(pl.multiple_of((1 - core) * row_count, row_count), row_count)
    normed_ref[other_rows] = norm_rows(other_ref[...], gain_ref[...])
    for index, out_ref in enumerate(outs):
        piece_width = out_ref.shape[1]
        offset = jnp.where(core == 0, orders[0][index] % len(outs), orders[1][index] % len(outs))
        start = pl.multiple_of((piece_ref[0] ^ offset) * piece_width, piece_width)
        out_ref[...] = normed_ref[:, pl.ds(start, piece_width)]


def product_kernel(core_ref, rows_ref, own_ref, other_ref, out_ref):
    half = rows_ref.shape[1] // 2

    def run(low, high):
        total = jnp.dot(rows_ref[:, :half], low[...], preferred_element_type=jnp.float32)
        total += jnp.dot(rows_ref[:, half:], high[...], preferred_element_type=jnp.float32)
        out_ref[...] = total.astype(out_ref.dtype)

    @pl.when(core_ref[0] == 0)
    def _():
        run(own_ref, other_ref)

    @pl.when(core_ref[0] == 1)
    def _():
        run(other_ref, own_ref)


def sum_kernel(orders, core_ref, *rest):
    parts, (kept_ref, sent_ref, total_ref) = rest[:-3], rest[-3:]
    core = core_ref[0]
    for member, order in enumerate(orders):

        @pl.when(core == member)
        def _(order=order):
            for kind in range(2):
                chosen = [part for part, distance in zip(parts, order) if (distance < len(order)) == bool(kind)]
                total_ref[kind] = sum((part[...].astype(jnp.float32) for part in chosen), jnp.zeros(total_ref.shape[1:], jnp.float32))

    row_count = kept_ref.shape[1]
    kept_ref[...] = total_ref[:, pl.ds(pl.multiple_of(core * row_count, row_count), row_count)]
    sent_ref[...] = total_ref[:, pl.ds(pl.multiple_of((1 - core) * row_count, row_count), row_count)]


def finish_kernel(variant_ref, ids_ref, kept_ref, received_ref, cosine_ref, sine_ref, out_ref):
    row_count, column_count = out_ref.shape
    square = (row_count, row_count)
    diagonal = lax.broadcasted_iota(jnp.int32, square, 0) == lax.broadcasted_iota(jnp.int32, square, 1)
    ids = jnp.sum(jnp.where(diagonal, ids_ref[...], 0), axis=1, keepdims=True)
    near = ids == variant_ref[0]
    total = jnp.where(near, kept_ref[1] + received_ref[1], kept_ref[0] + received_ref[0])
    for head in range(column_count // HEAD):
        columns = slice(head * HEAD, (head + 1) * HEAD)
        block = total[:, columns]
        swapped = pltpu.roll(block, HEAD // 2, 1)
        out_ref[:, columns] = (block * cosine_ref[...] + swapped * sine_ref[...]).astype(out_ref.dtype)


def turn_factors(position):
    half_size = HEAD // 2
    frequency = rope_theta ** (-(jnp.arange(half_size, dtype=jnp.float32) * 2.0 / HEAD))
    angles = position.astype(jnp.float32)[:, None] * frequency[None, :]
    cosine, sine = jnp.cos(angles), jnp.sin(angles)
    return jnp.concatenate([cosine, cosine], axis=1), jnp.concatenate([-sine, sine], axis=1)


VMEM = pl.BlockSpec(memory_space=pltpu.VMEM)
SMEM = pl.BlockSpec(memory_space=pltpu.SMEM)
ANY = pl.BlockSpec(memory_space=pl.ANY)


def in_hbm(array):
    return pltpu.with_memory_space_constraint(array, pltpu.HBM)


def paired(
    hidden, norm_gain, base_weight, delta_codes, delta_scales, delta_zeros, variant_ids, positions
):
    row_count, width = hidden.shape
    device_count = lax.axis_size("variant")
    pieces = OWNERS // 2
    slice_rows, column_count = delta_codes.shape[2:]
    place = lax.axis_index("variant")
    core = lax.rem(place, 2)
    piece = lax.div(lax.rem(place, OWNERS), 2)
    variant = lax.div(place, OWNERS)
    swap = [(index, index ^ 1) for index in range(device_count)]
    orders = ((4, 5, 6, 0), (7, 2, 3, 1))
    steps = list(zip(*orders))
    routes = [
        [(index, index ^ (2 * distances[index % 2])) for index in range(device_count)] for distances in steps
    ]

    slice_shape, group_shape = (slice_rows, column_count), delta_scales.shape[2:]
    own_codes, own_scales, own_zeros = delta_codes[0, 0], delta_scales[0, 0], delta_zeros[0, 0]
    other_hidden = lax.ppermute(hidden, "variant", swap)
    normed, gains, own_weight = pl.pallas_call(
        front_kernel,
        out_shape=[
            jax.ShapeDtypeStruct((row_count, width), jnp.bfloat16),
            jax.ShapeDtypeStruct((1, width), jnp.float32),
            jax.ShapeDtypeStruct(slice_shape, jnp.bfloat16),
        ],
        in_specs=[SMEM] + [ANY] * 6,
        out_specs=[VMEM] * 3,
        scratch_shapes=[
            pltpu.VMEM((row_count, width), jnp.bfloat16),
            pltpu.VMEM((width,), jnp.bfloat16),
            pltpu.VMEM(slice_shape, jnp.bfloat16),
            pltpu.VMEM(group_shape, jnp.float32),
            pltpu.VMEM(group_shape, jnp.float32),
            pltpu.VMEM(slice_shape, jnp.bfloat16),
            pltpu.SemaphoreType.DMA((8,)),
        ],
        compiler_params=pltpu.CompilerParams(vmem_limit_bytes=16 << 20),
        name="front",
    )(
        lax.rem(place, OWNERS)[None],
        *[in_hbm(array) for array in (hidden, norm_gain, own_codes, own_scales, own_zeros, base_weight)],
    )
    other_hidden, normed = lax.optimization_barrier((other_hidden, normed))
    outgoing = pl.pallas_call(
        functools.partial(pieces_kernel, orders),
        out_shape=[jax.ShapeDtypeStruct((2 * row_count, width // pieces), jnp.bfloat16)] * len(steps),
        in_specs=[SMEM, SMEM, VMEM, VMEM, VMEM],
        out_specs=[VMEM] * len(steps),
        scratch_shapes=[pltpu.VMEM((2 * row_count, width), jnp.bfloat16)],
        compiler_params=pltpu.CompilerParams(vmem_limit_bytes=16 << 20),
        name="pieces",
    )(piece[None], core[None], normed, other_hidden, gains)
    *outgoing, own_weight = lax.optimization_barrier((*outgoing, own_weight))
    other_weight, positions = lax.optimization_barrier((lax.ppermute(own_weight, "variant", swap), positions))
    incoming = [lax.ppermute(rows, "variant", route) for rows, route in zip(outgoing, routes)]
    parts = [None] * len(steps)
    for step in range(len(steps)):
        product = pl.pallas_call(
            product_kernel,
            out_shape=jax.ShapeDtypeStruct((2 * row_count, column_count), jnp.bfloat16),
            in_specs=[SMEM, VMEM, VMEM, VMEM],
            out_specs=VMEM,
            compiler_params=pltpu.CompilerParams(vmem_limit_bytes=16 << 20),
            name="product",
        )(core[None], incoming[step], own_weight, other_weight)
        parts[step] = lax.ppermute(product, "variant", routes[step])
    kept, sent = pl.pallas_call(
        functools.partial(sum_kernel, orders),
        out_shape=[jax.ShapeDtypeStruct((2, row_count, column_count), jnp.float32)] * 2,
        in_specs=[SMEM] + [VMEM] * len(parts),
        out_specs=[VMEM] * 2,
        scratch_shapes=[pltpu.VMEM((2, 2 * row_count, column_count), jnp.float32)],
        compiler_params=pltpu.CompilerParams(vmem_limit_bytes=8 << 20),
        name="sum",
    )(core[None], *parts)
    received = lax.ppermute(sent, "variant", swap)
    cosine, sine = turn_factors(positions)
    return pl.pallas_call(
        finish_kernel,
        out_shape=jax.ShapeDtypeStruct((row_count, column_count), jnp.bfloat16),
        in_specs=[SMEM] + [VMEM] * 5,
        out_specs=VMEM,
        compiler_params=pltpu.CompilerParams(vmem_limit_bytes=8 << 20),
        name="finish",
    )(variant[None], variant_ids.T, kept, received, cosine, sine)


def solution(mesh):
    devices = mesh.shape["variant"]
    small = mesh.shape["tensor"] == 1 and devices == 2 * OWNERS
    per_device = paired if small else general
    in_specs = (
        P(("groups", "variant"), "tensor"),
        P("tensor"),
        P("tensor", None),
        P("tensor", ("groups", "variant"), None, None),
        P("tensor", ("groups", "variant"), None, None),
        P("tensor", ("groups", "variant"), None, None),
        P(("groups", "variant"), None),
        P(("groups", "variant")),
    )
    out_specs = P(("groups", "variant"), "tensor")
    return jax.shard_map(
        per_device, mesh=mesh, in_specs=in_specs, out_specs=out_specs, check_vma=False
    )
```

```python
import functools

import jax
import jax.numpy as jnp
from jax import lax
from jax.experimental import pallas as pl
from jax.experimental.pallas import tpu as pltpu
from jax.sharding import PartitionSpec as P

HEAD = 128
OWNERS = 8


rope_theta = 500000.0
epsilon = 1e-05


def rotate_keys(projected, position):
    row_count = projected.shape[0]
    head_count = projected.shape[1] // HEAD
    half_size = HEAD // 2
    per_head = projected.reshape(row_count, head_count, HEAD)
    frequency = rope_theta ** (-(jnp.arange(half_size, dtype=jnp.float32) * 2.0 / HEAD))
    angles = position.astype(jnp.float32)[:, None] * frequency[None, :]
    cosine = jnp.cos(angles)[:, None, :]
    sine = jnp.sin(angles)[:, None, :]
    first = per_head[:, :, :half_size]
    second = per_head[:, :, half_size:]
    turned = jnp.concatenate(
        [first * cosine - second * sine, second * cosine + first * sine], axis=2
    )
    return turned.reshape(row_count, head_count * HEAD).astype(jnp.bfloat16)


def dequantize(code_block, scale_block, zero_block):
    group_count = scale_block.shape[-2]
    leading_dims = code_block.shape[:-2]
    slice_rows = code_block.shape[-2]
    column_count = code_block.shape[-1]
    grouped = code_block.astype(jnp.float32).reshape(
        leading_dims + (group_count, slice_rows // group_count, column_count)
    )
    values = (grouped - zero_block[..., :, None, :]) * scale_block[..., :, None, :]
    return values.reshape(leading_dims + (slice_rows, column_count))


def general(
    hidden, norm_gain, base_weight, delta_codes, delta_scales, delta_zeros, variant_ids, positions
):
    row_count, half_width = hidden.shape
    device_count = lax.axis_size("variant")
    variant_count = device_count // OWNERS
    capacity = min(row_count, max(2, 2 * row_count // variant_count))
    slice_rows = delta_codes.shape[2]
    column_count = base_weight.shape[1]
    floats = hidden.astype(jnp.float32)
    local_squares = jnp.sum(floats * floats, axis=1)
    all_squares = lax.psum(local_squares, "tensor")
    full_width = half_width * lax.axis_size("tensor")
    normed = (
        floats
        * lax.rsqrt(all_squares / full_width + epsilon)[:, None]
        * norm_gain.astype(jnp.float32)[None, :]
    ).astype(jnp.bfloat16)
    chosen = variant_ids[:, 0]
    labels = jnp.arange(variant_count, dtype=jnp.int32)
    member = (chosen[:, None] == labels[None, :]).astype(jnp.int32)
    earlier = jnp.cumsum(member, axis=0) - member
    ranking = jnp.sum(earlier * member, axis=1)
    target_slot = chosen * capacity + ranking
    slot_labels = jnp.arange(variant_count * capacity, dtype=jnp.int32)
    placing = slot_labels[:, None] == target_slot[None, :]
    place_send = placing.astype(jnp.bfloat16).reshape(variant_count, capacity, row_count)
    place_back = placing.astype(jnp.float32)
    feature_pieces = normed.reshape(row_count, OWNERS, slice_rows)
    outgoing = jnp.einsum(
        "vcr,rjs->vjcs", place_send, feature_pieces, preferred_element_type=jnp.float32
    )
    outgoing = outgoing.astype(jnp.bfloat16).reshape(device_count, capacity, slice_rows)
    local_delta = dequantize(delta_codes[0, 0], delta_scales[0, 0], delta_zeros[0, 0]).astype(
        jnp.bfloat16
    )
    products = jnp.einsum(
        "acs,sk->ack",
        lax.all_to_all(outgoing, "variant", split_axis=0, concat_axis=0, tiled=True),
        local_delta,
        preferred_element_type=jnp.float32,
    )
    base_part = jnp.dot(normed, base_weight, preferred_element_type=jnp.float32)
    returned = lax.all_to_all(products, "variant", split_axis=0, concat_axis=0, tiled=True)
    summed = jnp.sum(returned.reshape(variant_count, OWNERS, capacity, column_count), axis=1)
    summed = summed.reshape(variant_count * capacity, column_count)
    delta_rows = jnp.einsum("sr,sk->rk", place_back, summed, precision=lax.Precision.HIGHEST)
    combined = lax.psum_scatter(base_part + delta_rows, "tensor", scatter_dimension=1, tiled=True)
    return rotate_keys(combined, positions)


def norm_kernel(rows_ref, gain_ref, out_ref, gains_ref, rows, gain, arrived):
    copies = [
        pltpu.make_async_copy(gain_ref, gain, arrived.at[0]),
        pltpu.make_async_copy(rows_ref, rows, arrived.at[1]),
    ]
    for copy in copies:
        copy.start()
    copies[0].wait()
    gains_ref[...] = gain[...].astype(jnp.float32).reshape(gains_ref.shape)
    copies[1].wait()
    out_ref[...] = norm_rows(rows[...], gains_ref[...])


def weight_kernel(
    core_ref,
    first_ref,
    own_codes,
    own_scales,
    own_zeros,
    base_ref,
    other_codes,
    other_scales,
    other_zeros,
    out_ref,
    codes,
    scales,
    zeros,
    base,
    arrived,
):
    slice_rows = codes.shape[0]
    core = core_ref[0]
    starts = [pl.multiple_of((1 - core) * slice_rows, slice_rows), pl.multiple_of(core * slice_rows, slice_rows)]
    first = first_ref[0] * slice_rows
    copies = [
        pltpu.make_async_copy(
            base_ref.at[pl.ds(pl.multiple_of(first + starts[0], slice_rows), slice_rows)], base.at[0], arrived.at[0]
        ),
        pltpu.make_async_copy(own_scales, scales, arrived.at[1]),
        pltpu.make_async_copy(own_zeros, zeros, arrived.at[2]),
        pltpu.make_async_copy(own_codes, codes, arrived.at[3]),
        pltpu.make_async_copy(
            base_ref.at[pl.ds(pl.multiple_of(first + starts[1], slice_rows), slice_rows)], base.at[1], arrived.at[4]
        ),
    ]
    for copy in copies:
        copy.start()
    group_count = scales.shape[0]
    size = slice_rows // group_count
    sources = [(other_codes, other_scales, other_zeros), (codes, scales, zeros)]
    for member, (member_codes, member_scales, member_zeros) in enumerate(sources):
        for copy in copies[1:] if member else copies[:1]:
            copy.wait()
        for group in range(group_count):
            rows = slice(group * size, (group + 1) * size)
            delta = member_codes[rows].astype(jnp.float32) - member_zeros[group : group + 1]
            delta = delta * member_scales[group : group + 1]
            target = pl.ds(pl.multiple_of(starts[member] + group * size, size), size)
            out_ref[target] = (base[member, rows].astype(jnp.float32) + delta).astype(jnp.bfloat16)


def norm_rows(rows, gain):
    floats = rows.astype(jnp.float32)
    mean_square = jnp.sum(floats * floats, axis=1, keepdims=True) / rows.shape[1]
    return (floats * lax.rsqrt(mean_square + epsilon) * gain).astype(jnp.bfloat16)


def pieces_kernel(orders, piece_ref, core_ref, own_ref, other_ref, gain_ref, *rest):
    outs, normed_ref = rest[:-1], rest[-1]
    row_count = own_ref.shape[0]
    core = core_ref[0]
    normed_ref[pl.ds(pl.multiple_of(core * row_count, row_count), row_count)] = own_ref[...]
    other_rows = pl.ds(pl.multiple_of((1 - core) * row_count, row_count), row_count)
    normed_ref[other_rows] = norm_rows(other_ref[...], gain_ref[...])
    for index, out_ref in enumerate(outs):
        piece_width = out_ref.shape[1]
        offset = jnp.where(core == 0, orders[0][index] % len(outs), orders[1][index] % len(outs))
        start = pl.multiple_of((piece_ref[0] ^ offset) * piece_width, piece_width)
        out_ref[...] = normed_ref[:, pl.ds(start, piece_width)]


def product_kernel(rows_ref, weight_ref, out_ref):
    out_ref[...] = jnp.dot(rows_ref[...], weight_ref[...], preferred_element_type=jnp.float32).astype(out_ref.dtype)


def sum_kernel(orders, core_ref, *rest):
    parts, (kept_ref, sent_ref, total_ref) = rest[:-3], rest[-3:]
    core = core_ref[0]
    for member, order in enumerate(orders):

        @pl.when(core == member)
        def _(order=order):
            for kind in range(2):
                chosen = [part for part, distance in zip(parts, order) if (distance < len(order)) == bool(kind)]
                total_ref[kind] = sum((part[...].astype(jnp.float32) for part in chosen), jnp.zeros(total_ref.shape[1:], jnp.float32))

    row_count = kept_ref.shape[1]
    kept_ref[...] = total_ref[:, pl.ds(pl.multiple_of(core * row_count, row_count), row_count)]
    sent_ref[...] = total_ref[:, pl.ds(pl.multiple_of((1 - core) * row_count, row_count), row_count)]


def finish_kernel(variant_ref, ids_ref, kept_ref, received_ref, cosine_ref, sine_ref, out_ref):
    row_count, column_count = out_ref.shape
    square = (row_count, row_count)
    diagonal = lax.broadcasted_iota(jnp.int32, square, 0) == lax.broadcasted_iota(jnp.int32, square, 1)
    ids = jnp.sum(jnp.where(diagonal, ids_ref[...], 0), axis=1, keepdims=True)
    near = ids == variant_ref[0]
    total = jnp.where(near, kept_ref[1] + received_ref[1], kept_ref[0] + received_ref[0])
    for head in range(column_count // HEAD):
        columns = slice(head * HEAD, (head + 1) * HEAD)
        block = total[:, columns]
        swapped = pltpu.roll(block, HEAD // 2, 1)
        out_ref[:, columns] = (block * cosine_ref[...] + swapped * sine_ref[...]).astype(out_ref.dtype)


def turn_factors(position):
    half_size = HEAD // 2
    frequency = rope_theta ** (-(jnp.arange(half_size, dtype=jnp.float32) * 2.0 / HEAD))
    angles = position.astype(jnp.float32)[:, None] * frequency[None, :]
    cosine, sine = jnp.cos(angles), jnp.sin(angles)
    return jnp.concatenate([cosine, cosine], axis=1), jnp.concatenate([-sine, sine], axis=1)


VMEM = pl.BlockSpec(memory_space=pltpu.VMEM)
SMEM = pl.BlockSpec(memory_space=pltpu.SMEM)
ANY = pl.BlockSpec(memory_space=pl.ANY)


def in_hbm(array):
    return pltpu.with_memory_space_constraint(array, pltpu.HBM)


def paired(
    hidden, norm_gain, base_weight, delta_codes, delta_scales, delta_zeros, variant_ids, positions
):
    row_count, width = hidden.shape
    device_count = lax.axis_size("variant")
    pieces = OWNERS // 2
    slice_rows, column_count = delta_codes.shape[2:]
    place = lax.axis_index("variant")
    core = lax.rem(place, 2)
    piece = lax.div(lax.rem(place, OWNERS), 2)
    variant = lax.div(place, OWNERS)
    swap = [(index, index ^ 1) for index in range(device_count)]
    orders = ((4, 5, 6, 0), (7, 2, 3, 1))
    steps = list(zip(*orders))

    def route(distances, cross):
        return [(index, (index ^ (2 * distances[index % 2])) ^ cross) for index in range(device_count)]

    slice_shape, group_shape = (slice_rows, column_count), delta_scales.shape[2:]
    own_codes, own_scales, own_zeros = delta_codes[0, 0], delta_scales[0, 0], delta_zeros[0, 0]
    other_hidden = lax.ppermute(hidden, "variant", swap)
    other_scales = lax.ppermute(own_scales, "variant", swap)
    other_zeros = lax.ppermute(own_zeros, "variant", swap)
    normed, gains = pl.pallas_call(
        norm_kernel,
        out_shape=[jax.ShapeDtypeStruct((row_count, width), jnp.bfloat16), jax.ShapeDtypeStruct((1, width), jnp.float32)],
        in_specs=[ANY] * 2,
        out_specs=[VMEM] * 2,
        scratch_shapes=[
            pltpu.VMEM((row_count, width), jnp.bfloat16),
            pltpu.VMEM((width,), jnp.bfloat16),
            pltpu.SemaphoreType.DMA((2,)),
        ],
        compiler_params=pltpu.CompilerParams(vmem_limit_bytes=16 << 20),
        name="norm",
    )(in_hbm(hidden), in_hbm(norm_gain))
    other_hidden, other_scales, other_zeros, codes, normed = lax.optimization_barrier(
        (other_hidden, other_scales, other_zeros, own_codes, normed)
    )
    other_codes = lax.ppermute(codes, "variant", swap)
    outgoing = pl.pallas_call(
        functools.partial(pieces_kernel, orders),
        out_shape=[jax.ShapeDtypeStruct((2 * row_count, width // pieces), jnp.bfloat16)] * len(steps),
        in_specs=[SMEM, SMEM, VMEM, VMEM, VMEM],
        out_specs=[VMEM] * len(steps),
        scratch_shapes=[pltpu.VMEM((2 * row_count, width), jnp.bfloat16)],
        compiler_params=pltpu.CompilerParams(vmem_limit_bytes=16 << 20),
        name="pieces",
    )(piece[None], core[None], normed, other_hidden, gains)
    weight = pl.pallas_call(
        weight_kernel,
        out_shape=jax.ShapeDtypeStruct((2 * slice_rows, column_count), jnp.bfloat16),
        in_specs=[SMEM, SMEM] + [ANY] * 4 + [VMEM] * 3,
        out_specs=VMEM,
        scratch_shapes=[
            pltpu.VMEM(slice_shape, jnp.bfloat16),
            pltpu.VMEM(group_shape, jnp.float32),
            pltpu.VMEM(group_shape, jnp.float32),
            pltpu.VMEM((2,) + slice_shape, jnp.bfloat16),
            pltpu.SemaphoreType.DMA((5,)),
        ],
        compiler_params=pltpu.CompilerParams(vmem_limit_bytes=16 << 20),
        name="weight",
    )(
        core[None],
        (piece * 2)[None],
        in_hbm(own_codes),
        in_hbm(own_scales),
        in_hbm(own_zeros),
        in_hbm(base_weight),
        other_codes,
        other_scales,
        other_zeros,
    )
    weight, positions = lax.optimization_barrier((weight, positions))
    incoming = [lax.ppermute(rows, "variant", route(distances, 0)) for rows, distances in zip(outgoing, steps)]
    parts = [None] * len(steps)
    for step in range(len(steps)):
        product = pl.pallas_call(
            product_kernel,
            out_shape=jax.ShapeDtypeStruct((2 * row_count, column_count), jnp.bfloat16),
            in_specs=[VMEM, VMEM],
            out_specs=VMEM,
            compiler_params=pltpu.CompilerParams(vmem_limit_bytes=16 << 20),
            name="product",
        )(incoming[step], weight)
        parts[step] = lax.ppermute(product, "variant", route(steps[step], 1))
    kept, sent = pl.pallas_call(
        functools.partial(sum_kernel, orders[::-1]),
        out_shape=[jax.ShapeDtypeStruct((2, row_count, column_count), jnp.float32)] * 2,
        in_specs=[SMEM] + [VMEM] * len(parts),
        out_specs=[VMEM] * 2,
        scratch_shapes=[pltpu.VMEM((2, 2 * row_count, column_count), jnp.float32)],
        compiler_params=pltpu.CompilerParams(vmem_limit_bytes=8 << 20),
        name="sum",
    )(core[None], *parts)
    received = lax.ppermute(sent, "variant", swap)
    cosine, sine = turn_factors(positions)
    return pl.pallas_call(
        finish_kernel,
        out_shape=jax.ShapeDtypeStruct((row_count, column_count), jnp.bfloat16),
        in_specs=[SMEM] + [VMEM] * 5,
        out_specs=VMEM,
        compiler_params=pltpu.CompilerParams(vmem_limit_bytes=8 << 20),
        name="finish",
    )(variant[None], variant_ids.T, kept, received, cosine, sine)


def solution(mesh):
    devices = mesh.shape["variant"]
    small = mesh.shape["tensor"] == 1 and devices == 2 * OWNERS
    per_device = paired if small else general
    in_specs = (
        P(("groups", "variant"), "tensor"),
        P("tensor"),
        P("tensor", None),
        P("tensor", ("groups", "variant"), None, None),
        P("tensor", ("groups", "variant"), None, None),
        P("tensor", ("groups", "variant"), None, None),
        P(("groups", "variant"), None),
        P(("groups", "variant")),
    )
    out_specs = P(("groups", "variant"), "tensor")
    return jax.shard_map(
        per_device, mesh=mesh, in_specs=in_specs, out_specs=out_specs, check_vma=False
    )
```

```python
import functools

import jax
import jax.numpy as jnp
from jax import lax
from jax.experimental import pallas as pl
from jax.experimental.pallas import tpu as pltpu
from jax.sharding import PartitionSpec as P

HEAD = 128
OWNERS = 8


rope_theta = 500000.0
epsilon = 1e-05


def rotate_keys(projected, position):
    row_count = projected.shape[0]
    head_count = projected.shape[1] // HEAD
    half_size = HEAD // 2
    per_head = projected.reshape(row_count, head_count, HEAD)
    frequency = rope_theta ** (-(jnp.arange(half_size, dtype=jnp.float32) * 2.0 / HEAD))
    angles = position.astype(jnp.float32)[:, None] * frequency[None, :]
    cosine = jnp.cos(angles)[:, None, :]
    sine = jnp.sin(angles)[:, None, :]
    first = per_head[:, :, :half_size]
    second = per_head[:, :, half_size:]
    turned = jnp.concatenate(
        [first * cosine - second * sine, second * cosine + first * sine], axis=2
    )
    return turned.reshape(row_count, head_count * HEAD).astype(jnp.bfloat16)


def dequantize(code_block, scale_block, zero_block):
    group_count = scale_block.shape[-2]
    leading_dims = code_block.shape[:-2]
    slice_rows = code_block.shape[-2]
    column_count = code_block.shape[-1]
    grouped = code_block.astype(jnp.float32).reshape(
        leading_dims + (group_count, slice_rows // group_count, column_count)
    )
    values = (grouped - zero_block[..., :, None, :]) * scale_block[..., :, None, :]
    return values.reshape(leading_dims + (slice_rows, column_count))


def general(
    hidden, norm_gain, base_weight, delta_codes, delta_scales, delta_zeros, variant_ids, positions
):
    row_count, half_width = hidden.shape
    device_count = lax.axis_size("variant")
    variant_count = device_count // OWNERS
    capacity = min(row_count, max(2, 2 * row_count // variant_count))
    slice_rows = delta_codes.shape[2]
    column_count = base_weight.shape[1]
    floats = hidden.astype(jnp.float32)
    local_squares = jnp.sum(floats * floats, axis=1)
    all_squares = lax.psum(local_squares, "tensor")
    full_width = half_width * lax.axis_size("tensor")
    normed = (
        floats
        * lax.rsqrt(all_squares / full_width + epsilon)[:, None]
        * norm_gain.astype(jnp.float32)[None, :]
    ).astype(jnp.bfloat16)
    chosen = variant_ids[:, 0]
    labels = jnp.arange(variant_count, dtype=jnp.int32)
    member = (chosen[:, None] == labels[None, :]).astype(jnp.int32)
    earlier = jnp.cumsum(member, axis=0) - member
    ranking = jnp.sum(earlier * member, axis=1)
    target_slot = chosen * capacity + ranking
    slot_labels = jnp.arange(variant_count * capacity, dtype=jnp.int32)
    placing = slot_labels[:, None] == target_slot[None, :]
    place_send = placing.astype(jnp.bfloat16).reshape(variant_count, capacity, row_count)
    place_back = placing.astype(jnp.float32)
    feature_pieces = normed.reshape(row_count, OWNERS, slice_rows)
    outgoing = jnp.einsum(
        "vcr,rjs->vjcs", place_send, feature_pieces, preferred_element_type=jnp.float32
    )
    outgoing = outgoing.astype(jnp.bfloat16).reshape(device_count, capacity, slice_rows)
    local_delta = dequantize(delta_codes[0, 0], delta_scales[0, 0], delta_zeros[0, 0]).astype(
        jnp.bfloat16
    )
    products = jnp.einsum(
        "acs,sk->ack",
        lax.all_to_all(outgoing, "variant", split_axis=0, concat_axis=0, tiled=True),
        local_delta,
        preferred_element_type=jnp.float32,
    )
    base_part = jnp.dot(normed, base_weight, preferred_element_type=jnp.float32)
    returned = lax.all_to_all(products, "variant", split_axis=0, concat_axis=0, tiled=True)
    summed = jnp.sum(returned.reshape(variant_count, OWNERS, capacity, column_count), axis=1)
    summed = summed.reshape(variant_count * capacity, column_count)
    delta_rows = jnp.einsum("sr,sk->rk", place_back, summed, precision=lax.Precision.HIGHEST)
    combined = lax.psum_scatter(base_part + delta_rows, "tensor", scatter_dimension=1, tiled=True)
    return rotate_keys(combined, positions)


def norm_kernel(rows_ref, gain_ref, out_ref, gains_ref, rows, gain, arrived):
    copies = [
        pltpu.make_async_copy(gain_ref, gain, arrived.at[0]),
        pltpu.make_async_copy(rows_ref, rows, arrived.at[1]),
    ]
    for copy in copies:
        copy.start()
    copies[0].wait()
    gains_ref[...] = gain[...].astype(jnp.float32).reshape(gains_ref.shape)
    copies[1].wait()
    out_ref[...] = norm_rows(rows[...], gains_ref[...])


def weight_kernel(
    core_ref,
    first_ref,
    own_codes,
    own_scales,
    own_zeros,
    base_ref,
    other_codes,
    other_scales,
    other_zeros,
    out_ref,
    codes,
    scales,
    zeros,
    base,
    arrived,
):
    slice_rows = codes.shape[0]
    core = core_ref[0]
    starts = [pl.multiple_of((1 - core) * slice_rows, slice_rows), pl.multiple_of(core * slice_rows, slice_rows)]
    first = first_ref[0] * slice_rows
    copies = [
        pltpu.make_async_copy(
            base_ref.at[pl.ds(pl.multiple_of(first + starts[0], slice_rows), slice_rows)], base.at[0], arrived.at[0]
        ),
        pltpu.make_async_copy(own_scales, scales, arrived.at[1]),
        pltpu.make_async_copy(own_zeros, zeros, arrived.at[2]),
        pltpu.make_async_copy(own_codes, codes, arrived.at[3]),
        pltpu.make_async_copy(
            base_ref.at[pl.ds(pl.multiple_of(first + starts[1], slice_rows), slice_rows)], base.at[1], arrived.at[4]
        ),
    ]
    for copy in copies:
        copy.start()
    group_count = scales.shape[0]
    size = slice_rows // group_count
    sources = [(other_codes, other_scales, other_zeros), (codes, scales, zeros)]
    for member, (member_codes, member_scales, member_zeros) in enumerate(sources):
        for copy in copies[1:] if member else copies[:1]:
            copy.wait()
        for group in range(group_count):
            rows = slice(group * size, (group + 1) * size)
            delta = member_codes[rows].astype(jnp.float32) - member_zeros[group : group + 1]
            delta = delta * member_scales[group : group + 1]
            target = pl.ds(pl.multiple_of(starts[member] + group * size, size), size)
            out_ref[target] = (base[member, rows].astype(jnp.float32) + delta).astype(jnp.bfloat16)


def norm_rows(rows, gain):
    floats = rows.astype(jnp.float32)
    mean_square = jnp.sum(floats * floats, axis=1, keepdims=True) / rows.shape[1]
    return (floats * lax.rsqrt(mean_square + epsilon) * gain).astype(jnp.bfloat16)


def pieces_kernel(orders, piece_ref, core_ref, own_ref, other_ref, gain_ref, *rest):
    outs, normed_ref = rest[:-1], rest[-1]
    row_count = own_ref.shape[0]
    core = core_ref[0]
    normed_ref[pl.ds(pl.multiple_of(core * row_count, row_count), row_count)] = own_ref[...]
    other_rows = pl.ds(pl.multiple_of((1 - core) * row_count, row_count), row_count)
    normed_ref[other_rows] = norm_rows(other_ref[...], gain_ref[...])
    for index, out_ref in enumerate(outs):
        piece_width = out_ref.shape[1]
        offset = jnp.where(core == 0, orders[0][index] % len(outs), orders[1][index] % len(outs))
        start = pl.multiple_of((piece_ref[0] ^ offset) * piece_width, piece_width)
        out_ref[...] = normed_ref[:, pl.ds(start, piece_width)]


def product_kernel(rows_ref, weight_ref, out_ref):
    out_ref[...] = jnp.dot(rows_ref[...], weight_ref[...], preferred_element_type=jnp.float32).astype(out_ref.dtype)


def sum_kernel(orders, core_ref, *rest):
    parts, (kept_ref, sent_ref, total_ref) = rest[:-3], rest[-3:]
    core = core_ref[0]
    for member, order in enumerate(orders):

        @pl.when(core == member)
        def _(order=order):
            for kind in range(2):
                chosen = [part for part, distance in zip(parts, order) if (distance < len(order)) == bool(kind)]
                total_ref[kind] = sum((part[...].astype(jnp.float32) for part in chosen), jnp.zeros(total_ref.shape[1:], jnp.float32))

    row_count = kept_ref.shape[1]
    kept_ref[...] = total_ref[:, pl.ds(pl.multiple_of(core * row_count, row_count), row_count)]
    sent_ref[...] = total_ref[:, pl.ds(pl.multiple_of((1 - core) * row_count, row_count), row_count)]


def finish_kernel(variant_ref, ids_ref, kept_ref, received_ref, cosine_ref, sine_ref, out_ref):
    row_count, column_count = out_ref.shape
    square = (row_count, row_count)
    diagonal = lax.broadcasted_iota(jnp.int32, square, 0) == lax.broadcasted_iota(jnp.int32, square, 1)
    ids = jnp.sum(jnp.where(diagonal, ids_ref[...], 0), axis=1, keepdims=True)
    near = ids == variant_ref[0]
    total = jnp.where(near, kept_ref[1] + received_ref[1], kept_ref[0] + received_ref[0])
    for head in range(column_count // HEAD):
        columns = slice(head * HEAD, (head + 1) * HEAD)
        block = total[:, columns]
        swapped = pltpu.roll(block, HEAD // 2, 1)
        out_ref[:, columns] = (block * cosine_ref[...] + swapped * sine_ref[...]).astype(out_ref.dtype)


def turn_factors(position):
    half_size = HEAD // 2
    frequency = rope_theta ** (-(jnp.arange(half_size, dtype=jnp.float32) * 2.0 / HEAD))
    angles = position.astype(jnp.float32)[:, None] * frequency[None, :]
    cosine, sine = jnp.cos(angles), jnp.sin(angles)
    return jnp.concatenate([cosine, cosine], axis=1), jnp.concatenate([-sine, sine], axis=1)


VMEM = pl.BlockSpec(memory_space=pltpu.VMEM)
SMEM = pl.BlockSpec(memory_space=pltpu.SMEM)
ANY = pl.BlockSpec(memory_space=pl.ANY)


def in_hbm(array):
    return pltpu.with_memory_space_constraint(array, pltpu.HBM)


def paired(
    hidden, norm_gain, base_weight, delta_codes, delta_scales, delta_zeros, variant_ids, positions
):
    row_count, width = hidden.shape
    device_count = lax.axis_size("variant")
    pieces = OWNERS // 2
    slice_rows, column_count = delta_codes.shape[2:]
    place = lax.axis_index("variant")
    core = lax.rem(place, 2)
    piece = lax.div(lax.rem(place, OWNERS), 2)
    variant = lax.div(place, OWNERS)
    swap = [(index, index ^ 1) for index in range(device_count)]
    orders = ((7, 5, 4, 0), (6, 3, 2, 1))
    steps = list(zip(*orders))

    def route(distances, cross):
        return [(index, (index ^ (2 * distances[index % 2])) ^ cross) for index in range(device_count)]

    slice_shape, group_shape = (slice_rows, column_count), delta_scales.shape[2:]
    own_codes, own_scales, own_zeros = delta_codes[0, 0], delta_scales[0, 0], delta_zeros[0, 0]
    other_hidden = lax.ppermute(hidden, "variant", swap)
    other_scales = lax.ppermute(own_scales, "variant", swap)
    other_zeros = lax.ppermute(own_zeros, "variant", swap)
    normed, gains = pl.pallas_call(
        norm_kernel,
        out_shape=[jax.ShapeDtypeStruct((row_count, width), jnp.bfloat16), jax.ShapeDtypeStruct((1, width), jnp.float32)],
        in_specs=[ANY] * 2,
        out_specs=[VMEM] * 2,
        scratch_shapes=[
            pltpu.VMEM((row_count, width), jnp.bfloat16),
            pltpu.VMEM((width,), jnp.bfloat16),
            pltpu.SemaphoreType.DMA((2,)),
        ],
        compiler_params=pltpu.CompilerParams(vmem_limit_bytes=16 << 20),
        name="norm",
    )(in_hbm(hidden), in_hbm(norm_gain))
    other_hidden, other_scales, other_zeros, codes, normed = lax.optimization_barrier(
        (other_hidden, other_scales, other_zeros, own_codes, normed)
    )
    other_codes = lax.ppermute(codes, "variant", swap)
    outgoing = pl.pallas_call(
        functools.partial(pieces_kernel, orders),
        out_shape=[jax.ShapeDtypeStruct((2 * row_count, width // pieces), jnp.bfloat16)] * len(steps),
        in_specs=[SMEM, SMEM, VMEM, VMEM, VMEM],
        out_specs=[VMEM] * len(steps),
        scratch_shapes=[pltpu.VMEM((2 * row_count, width), jnp.bfloat16)],
        compiler_params=pltpu.CompilerParams(vmem_limit_bytes=16 << 20),
        name="pieces",
    )(piece[None], core[None], normed, other_hidden, gains)
    weight = pl.pallas_call(
        weight_kernel,
        out_shape=jax.ShapeDtypeStruct((2 * slice_rows, column_count), jnp.bfloat16),
        in_specs=[SMEM, SMEM] + [ANY] * 4 + [VMEM] * 3,
        out_specs=VMEM,
        scratch_shapes=[
            pltpu.VMEM(slice_shape, jnp.bfloat16),
            pltpu.VMEM(group_shape, jnp.float32),
            pltpu.VMEM(group_shape, jnp.float32),
            pltpu.VMEM((2,) + slice_shape, jnp.bfloat16),
            pltpu.SemaphoreType.DMA((5,)),
        ],
        compiler_params=pltpu.CompilerParams(vmem_limit_bytes=16 << 20),
        name="weight",
    )(
        core[None],
        (piece * 2)[None],
        in_hbm(own_codes),
        in_hbm(own_scales),
        in_hbm(own_zeros),
        in_hbm(base_weight),
        other_codes,
        other_scales,
        other_zeros,
    )
    weight, positions = lax.optimization_barrier((weight, positions))
    incoming = [lax.ppermute(rows, "variant", route(distances, 0)) for rows, distances in zip(outgoing, steps)]
    parts = [None] * len(steps)
    for step in range(len(steps)):
        product = pl.pallas_call(
            product_kernel,
            out_shape=jax.ShapeDtypeStruct((2 * row_count, column_count), jnp.bfloat16),
            in_specs=[VMEM, VMEM],
            out_specs=VMEM,
            compiler_params=pltpu.CompilerParams(vmem_limit_bytes=16 << 20),
            name="product",
        )(incoming[step], weight)
        parts[step] = lax.ppermute(product, "variant", route(steps[step], 1))
    kept, sent = pl.pallas_call(
        functools.partial(sum_kernel, orders[::-1]),
        out_shape=[jax.ShapeDtypeStruct((2, row_count, column_count), jnp.float32)] * 2,
        in_specs=[SMEM] + [VMEM] * len(parts),
        out_specs=[VMEM] * 2,
        scratch_shapes=[pltpu.VMEM((2, 2 * row_count, column_count), jnp.float32)],
        compiler_params=pltpu.CompilerParams(vmem_limit_bytes=8 << 20),
        name="sum",
    )(core[None], *parts)
    received = lax.ppermute(sent, "variant", swap)
    cosine, sine = turn_factors(positions)
    return pl.pallas_call(
        finish_kernel,
        out_shape=jax.ShapeDtypeStruct((row_count, column_count), jnp.bfloat16),
        in_specs=[SMEM] + [VMEM] * 5,
        out_specs=VMEM,
        compiler_params=pltpu.CompilerParams(vmem_limit_bytes=8 << 20),
        name="finish",
    )(variant[None], variant_ids.T, kept, received, cosine, sine)


def solution(mesh):
    devices = mesh.shape["variant"]
    small = mesh.shape["tensor"] == 1 and devices == 2 * OWNERS
    per_device = paired if small else general
    in_specs = (
        P(("groups", "variant"), "tensor"),
        P("tensor"),
        P("tensor", None),
        P("tensor", ("groups", "variant"), None, None),
        P("tensor", ("groups", "variant"), None, None),
        P("tensor", ("groups", "variant"), None, None),
        P(("groups", "variant"), None),
        P(("groups", "variant")),
    )
    out_specs = P(("groups", "variant"), "tensor")
    return jax.shard_map(
        per_device, mesh=mesh, in_specs=in_specs, out_specs=out_specs, check_vma=False
    )
```

```python
import functools

import jax
import jax.numpy as jnp
from jax import lax
from jax.experimental import pallas as pl
from jax.experimental.pallas import tpu as pltpu
from jax.sharding import PartitionSpec as P

HEAD = 128
OWNERS = 8


rope_theta = 500000.0
epsilon = 1e-05


def rotate_keys(projected, position):
    row_count = projected.shape[0]
    head_count = projected.shape[1] // HEAD
    half_size = HEAD // 2
    per_head = projected.reshape(row_count, head_count, HEAD)
    frequency = rope_theta ** (-(jnp.arange(half_size, dtype=jnp.float32) * 2.0 / HEAD))
    angles = position.astype(jnp.float32)[:, None] * frequency[None, :]
    cosine = jnp.cos(angles)[:, None, :]
    sine = jnp.sin(angles)[:, None, :]
    first = per_head[:, :, :half_size]
    second = per_head[:, :, half_size:]
    turned = jnp.concatenate(
        [first * cosine - second * sine, second * cosine + first * sine], axis=2
    )
    return turned.reshape(row_count, head_count * HEAD).astype(jnp.bfloat16)


def dequantize(code_block, scale_block, zero_block):
    group_count = scale_block.shape[-2]
    leading_dims = code_block.shape[:-2]
    slice_rows = code_block.shape[-2]
    column_count = code_block.shape[-1]
    grouped = code_block.astype(jnp.float32).reshape(
        leading_dims + (group_count, slice_rows // group_count, column_count)
    )
    values = (grouped - zero_block[..., :, None, :]) * scale_block[..., :, None, :]
    return values.reshape(leading_dims + (slice_rows, column_count))


def general(
    hidden, norm_gain, base_weight, delta_codes, delta_scales, delta_zeros, variant_ids, positions
):
    row_count, half_width = hidden.shape
    device_count = lax.axis_size("variant")
    variant_count = device_count // OWNERS
    capacity = min(row_count, max(2, 2 * row_count // variant_count))
    slice_rows = delta_codes.shape[2]
    column_count = base_weight.shape[1]
    floats = hidden.astype(jnp.float32)
    local_squares = jnp.sum(floats * floats, axis=1)
    all_squares = lax.psum(local_squares, "tensor")
    full_width = half_width * lax.axis_size("tensor")
    normed = (
        floats
        * lax.rsqrt(all_squares / full_width + epsilon)[:, None]
        * norm_gain.astype(jnp.float32)[None, :]
    ).astype(jnp.bfloat16)
    chosen = variant_ids[:, 0]
    labels = jnp.arange(variant_count, dtype=jnp.int32)
    member = (chosen[:, None] == labels[None, :]).astype(jnp.int32)
    earlier = jnp.cumsum(member, axis=0) - member
    ranking = jnp.sum(earlier * member, axis=1)
    target_slot = chosen * capacity + ranking
    slot_labels = jnp.arange(variant_count * capacity, dtype=jnp.int32)
    placing = slot_labels[:, None] == target_slot[None, :]
    place_send = placing.astype(jnp.bfloat16).reshape(variant_count, capacity, row_count)
    place_back = placing.astype(jnp.float32)
    feature_pieces = normed.reshape(row_count, OWNERS, slice_rows)
    outgoing = jnp.einsum(
        "vcr,rjs->vjcs", place_send, feature_pieces, preferred_element_type=jnp.float32
    )
    outgoing = outgoing.astype(jnp.bfloat16).reshape(device_count, capacity, slice_rows)
    local_delta = dequantize(delta_codes[0, 0], delta_scales[0, 0], delta_zeros[0, 0]).astype(
        jnp.bfloat16
    )
    products = jnp.einsum(
        "acs,sk->ack",
        lax.all_to_all(outgoing, "variant", split_axis=0, concat_axis=0, tiled=True),
        local_delta,
        preferred_element_type=jnp.float32,
    )
    base_part = jnp.dot(normed, base_weight, preferred_element_type=jnp.float32)
    returned = lax.all_to_all(products, "variant", split_axis=0, concat_axis=0, tiled=True)
    summed = jnp.sum(returned.reshape(variant_count, OWNERS, capacity, column_count), axis=1)
    summed = summed.reshape(variant_count * capacity, column_count)
    delta_rows = jnp.einsum("sr,sk->rk", place_back, summed, precision=lax.Precision.HIGHEST)
    combined = lax.psum_scatter(base_part + delta_rows, "tensor", scatter_dimension=1, tiled=True)
    return rotate_keys(combined, positions)


def norm_kernel(rows_ref, gain_ref, out_ref, gains_ref, rows, gain, arrived):
    copies = [
        pltpu.make_async_copy(gain_ref, gain, arrived.at[0]),
        pltpu.make_async_copy(rows_ref, rows, arrived.at[1]),
    ]
    for copy in copies:
        copy.start()
    copies[0].wait()
    gains_ref[...] = gain[...].astype(jnp.float32).reshape(gains_ref.shape)
    copies[1].wait()
    out_ref[...] = norm_rows(rows[...], gains_ref[...])


def weight_kernel(
    core_ref,
    first_ref,
    own_codes,
    own_scales,
    own_zeros,
    base_ref,
    other_codes,
    other_scales,
    other_zeros,
    out_ref,
    codes,
    scales,
    zeros,
    base,
    arrived,
):
    slice_rows = codes.shape[0]
    core = core_ref[0]
    starts = [pl.multiple_of((1 - core) * slice_rows, slice_rows), pl.multiple_of(core * slice_rows, slice_rows)]
    first = first_ref[0] * slice_rows
    copies = [
        pltpu.make_async_copy(
            base_ref.at[pl.ds(pl.multiple_of(first + starts[0], slice_rows), slice_rows)], base.at[0], arrived.at[0]
        ),
        pltpu.make_async_copy(own_scales, scales, arrived.at[1]),
        pltpu.make_async_copy(own_zeros, zeros, arrived.at[2]),
        pltpu.make_async_copy(own_codes, codes, arrived.at[3]),
        pltpu.make_async_copy(
            base_ref.at[pl.ds(pl.multiple_of(first + starts[1], slice_rows), slice_rows)], base.at[1], arrived.at[4]
        ),
    ]
    for copy in copies:
        copy.start()
    group_count = scales.shape[0]
    size = slice_rows // group_count
    sources = [(other_codes, other_scales, other_zeros), (codes, scales, zeros)]
    for member, (member_codes, member_scales, member_zeros) in enumerate(sources):
        for copy in copies[1:] if member else copies[:1]:
            copy.wait()
        for group in range(group_count):
            rows = slice(group * size, (group + 1) * size)
            delta = member_codes[rows].astype(jnp.float32) - member_zeros[group : group + 1]
            delta = delta * member_scales[group : group + 1]
            target = pl.ds(pl.multiple_of(starts[member] + group * size, size), size)
            out_ref[target] = (base[member, rows].astype(jnp.float32) + delta).astype(jnp.bfloat16)


def norm_rows(rows, gain):
    floats = rows.astype(jnp.float32)
    mean_square = jnp.sum(floats * floats, axis=1, keepdims=True) / rows.shape[1]
    return (floats * lax.rsqrt(mean_square + epsilon) * gain).astype(jnp.bfloat16)


def pieces_kernel(orders, piece_ref, core_ref, own_ref, other_ref, gain_ref, *rest):
    outs, normed_ref = rest[:-1], rest[-1]
    row_count = own_ref.shape[0]
    core = core_ref[0]
    normed_ref[pl.ds(pl.multiple_of(core * row_count, row_count), row_count)] = own_ref[...]
    other_rows = pl.ds(pl.multiple_of((1 - core) * row_count, row_count), row_count)
    normed_ref[other_rows] = norm_rows(other_ref[...], gain_ref[...])
    for index, out_ref in enumerate(outs):
        piece_width = out_ref.shape[1]
        offset = jnp.where(core == 0, orders[0][index] % len(outs), orders[1][index] % len(outs))
        start = pl.multiple_of((piece_ref[0] ^ offset) * piece_width, piece_width)
        out_ref[...] = normed_ref[:, pl.ds(start, piece_width)]


def product_kernel(rows_ref, weight_ref, out_ref):
    out_ref[...] = jnp.dot(rows_ref[...], weight_ref[...], preferred_element_type=jnp.float32).astype(out_ref.dtype)


def sum_kernel(orders, core_ref, *rest):
    parts, (kept_ref, sent_ref, total_ref) = rest[:-3], rest[-3:]
    core = core_ref[0]
    for member, order in enumerate(orders):

        @pl.when(core == member)
        def _(order=order):
            for kind in range(2):
                chosen = [part for part, distance in zip(parts, order) if (distance < len(order)) == bool(kind)]
                total_ref[kind] = sum((part[...].astype(jnp.float32) for part in chosen), jnp.zeros(total_ref.shape[1:], jnp.float32))

    row_count = kept_ref.shape[1]
    kept_ref[...] = total_ref[:, pl.ds(pl.multiple_of(core * row_count, row_count), row_count)]
    sent_ref[...] = total_ref[:, pl.ds(pl.multiple_of((1 - core) * row_count, row_count), row_count)]


def finish_kernel(variant_ref, ids_ref, kept_ref, received_ref, cosine_ref, sine_ref, out_ref):
    row_count, column_count = out_ref.shape
    square = (row_count, row_count)
    diagonal = lax.broadcasted_iota(jnp.int32, square, 0) == lax.broadcasted_iota(jnp.int32, square, 1)
    ids = jnp.sum(jnp.where(diagonal, ids_ref[...], 0), axis=1, keepdims=True)
    near = ids == variant_ref[0]
    total = jnp.where(near, kept_ref[1] + received_ref[1], kept_ref[0] + received_ref[0])
    for head in range(column_count // HEAD):
        columns = slice(head * HEAD, (head + 1) * HEAD)
        block = total[:, columns]
        swapped = pltpu.roll(block, HEAD // 2, 1)
        out_ref[:, columns] = (block * cosine_ref[...] + swapped * sine_ref[...]).astype(out_ref.dtype)


def turn_factors(position):
    half_size = HEAD // 2
    frequency = rope_theta ** (-(jnp.arange(half_size, dtype=jnp.float32) * 2.0 / HEAD))
    angles = position.astype(jnp.float32)[:, None] * frequency[None, :]
    cosine, sine = jnp.cos(angles), jnp.sin(angles)
    return jnp.concatenate([cosine, cosine], axis=1), jnp.concatenate([-sine, sine], axis=1)


VMEM = pl.BlockSpec(memory_space=pltpu.VMEM)
SMEM = pl.BlockSpec(memory_space=pltpu.SMEM)
ANY = pl.BlockSpec(memory_space=pl.ANY)


def in_hbm(array):
    return pltpu.with_memory_space_constraint(array, pltpu.HBM)


def paired(
    hidden, norm_gain, base_weight, delta_codes, delta_scales, delta_zeros, variant_ids, positions
):
    row_count, width = hidden.shape
    device_count = lax.axis_size("variant")
    pieces = OWNERS // 2
    slice_rows, column_count = delta_codes.shape[2:]
    place = lax.axis_index("variant")
    core = lax.rem(place, 2)
    piece = lax.div(lax.rem(place, OWNERS), 2)
    variant = lax.div(place, OWNERS)
    swap = [(index, index ^ 1) for index in range(device_count)]
    orders = ((7, 5, 4, 0), (6, 3, 2, 1))
    steps = list(zip(*orders))

    crossed = (0, 0, 1, 0)

    def route(distances, cross, turned=0):
        return [(index, (index ^ (2 * distances[(index % 2) ^ turned])) ^ cross) for index in range(device_count)]

    slice_shape, group_shape = (slice_rows, column_count), delta_scales.shape[2:]
    own_codes, own_scales, own_zeros = delta_codes[0, 0], delta_scales[0, 0], delta_zeros[0, 0]
    other_hidden = lax.ppermute(hidden, "variant", swap)
    other_scales = lax.ppermute(own_scales, "variant", swap)
    other_zeros = lax.ppermute(own_zeros, "variant", swap)
    normed, gains = pl.pallas_call(
        norm_kernel,
        out_shape=[jax.ShapeDtypeStruct((row_count, width), jnp.bfloat16), jax.ShapeDtypeStruct((1, width), jnp.float32)],
        in_specs=[ANY] * 2,
        out_specs=[VMEM] * 2,
        scratch_shapes=[
            pltpu.VMEM((row_count, width), jnp.bfloat16),
            pltpu.VMEM((width,), jnp.bfloat16),
            pltpu.SemaphoreType.DMA((2,)),
        ],
        compiler_params=pltpu.CompilerParams(vmem_limit_bytes=16 << 20),
        name="norm",
    )(in_hbm(hidden), in_hbm(norm_gain))
    other_hidden, other_scales, other_zeros, codes, normed = lax.optimization_barrier(
        (other_hidden, other_scales, other_zeros, own_codes, normed)
    )
    other_codes = lax.ppermute(codes, "variant", swap)
    outgoing = pl.pallas_call(
        functools.partial(pieces_kernel, orders),
        out_shape=[jax.ShapeDtypeStruct((2 * row_count, width // pieces), jnp.bfloat16)] * len(steps),
        in_specs=[SMEM, SMEM, VMEM, VMEM, VMEM],
        out_specs=[VMEM] * len(steps),
        scratch_shapes=[pltpu.VMEM((2 * row_count, width), jnp.bfloat16)],
        compiler_params=pltpu.CompilerParams(vmem_limit_bytes=16 << 20),
        name="pieces",
    )(piece[None], core[None], normed, other_hidden, gains)
    weight = pl.pallas_call(
        weight_kernel,
        out_shape=jax.ShapeDtypeStruct((2 * slice_rows, column_count), jnp.bfloat16),
        in_specs=[SMEM, SMEM] + [ANY] * 4 + [VMEM] * 3,
        out_specs=VMEM,
        scratch_shapes=[
            pltpu.VMEM(slice_shape, jnp.bfloat16),
            pltpu.VMEM(group_shape, jnp.float32),
            pltpu.VMEM(group_shape, jnp.float32),
            pltpu.VMEM((2,) + slice_shape, jnp.bfloat16),
            pltpu.SemaphoreType.DMA((5,)),
        ],
        compiler_params=pltpu.CompilerParams(vmem_limit_bytes=16 << 20),
        name="weight",
    )(
        core[None],
        (piece * 2)[None],
        in_hbm(own_codes),
        in_hbm(own_scales),
        in_hbm(own_zeros),
        in_hbm(base_weight),
        other_codes,
        other_scales,
        other_zeros,
    )
    weight, positions = lax.optimization_barrier((weight, positions))
    incoming = [lax.ppermute(rows, "variant", route(distances, cross)) for rows, distances, cross in zip(outgoing, steps, crossed)]
    parts = [None] * len(steps)
    for step in range(len(steps)):
        product = pl.pallas_call(
            product_kernel,
            out_shape=jax.ShapeDtypeStruct((2 * row_count, column_count), jnp.bfloat16),
            in_specs=[VMEM, VMEM],
            out_specs=VMEM,
            compiler_params=pltpu.CompilerParams(vmem_limit_bytes=16 << 20),
            name="product",
        )(incoming[step], weight)
        parts[step] = lax.ppermute(product, "variant", route(steps[step], 1 ^ crossed[step], crossed[step]))
    kept, sent = pl.pallas_call(
        functools.partial(sum_kernel, orders[::-1]),
        out_shape=[jax.ShapeDtypeStruct((2, row_count, column_count), jnp.float32)] * 2,
        in_specs=[SMEM] + [VMEM] * len(parts),
        out_specs=[VMEM] * 2,
        scratch_shapes=[pltpu.VMEM((2, 2 * row_count, column_count), jnp.float32)],
        compiler_params=pltpu.CompilerParams(vmem_limit_bytes=8 << 20),
        name="sum",
    )(core[None], *parts)
    received = lax.ppermute(sent, "variant", swap)
    cosine, sine = turn_factors(positions)
    return pl.pallas_call(
        finish_kernel,
        out_shape=jax.ShapeDtypeStruct((row_count, column_count), jnp.bfloat16),
        in_specs=[SMEM] + [VMEM] * 5,
        out_specs=VMEM,
        compiler_params=pltpu.CompilerParams(vmem_limit_bytes=8 << 20),
        name="finish",
    )(variant[None], variant_ids.T, kept, received, cosine, sine)


def solution(mesh):
    devices = mesh.shape["variant"]
    small = mesh.shape["tensor"] == 1 and devices == 2 * OWNERS
    per_device = paired if small else general
    in_specs = (
        P(("groups", "variant"), "tensor"),
        P("tensor"),
        P("tensor", None),
        P("tensor", ("groups", "variant"), None, None),
        P("tensor", ("groups", "variant"), None, None),
        P("tensor", ("groups", "variant"), None, None),
        P(("groups", "variant"), None),
        P(("groups", "variant")),
    )
    out_specs = P(("groups", "variant"), "tensor")
    return jax.shard_map(
        per_device, mesh=mesh, in_specs=in_specs, out_specs=out_specs, check_vma=False
    )
```

```python
import functools

import jax
import jax.numpy as jnp
from jax import lax
from jax.experimental import pallas as pl
from jax.experimental.pallas import tpu as pltpu
from jax.sharding import PartitionSpec as P

HEAD = 128
OWNERS = 8


rope_theta = 500000.0
epsilon = 1e-05


def rotate_keys(projected, position):
    row_count = projected.shape[0]
    head_count = projected.shape[1] // HEAD
    half_size = HEAD // 2
    per_head = projected.reshape(row_count, head_count, HEAD)
    frequency = rope_theta ** (-(jnp.arange(half_size, dtype=jnp.float32) * 2.0 / HEAD))
    angles = position.astype(jnp.float32)[:, None] * frequency[None, :]
    cosine = jnp.cos(angles)[:, None, :]
    sine = jnp.sin(angles)[:, None, :]
    first = per_head[:, :, :half_size]
    second = per_head[:, :, half_size:]
    turned = jnp.concatenate(
        [first * cosine - second * sine, second * cosine + first * sine], axis=2
    )
    return turned.reshape(row_count, head_count * HEAD).astype(jnp.bfloat16)


def dequantize(code_block, scale_block, zero_block):
    group_count = scale_block.shape[-2]
    leading_dims = code_block.shape[:-2]
    slice_rows = code_block.shape[-2]
    column_count = code_block.shape[-1]
    grouped = code_block.astype(jnp.float32).reshape(
        leading_dims + (group_count, slice_rows // group_count, column_count)
    )
    values = (grouped - zero_block[..., :, None, :]) * scale_block[..., :, None, :]
    return values.reshape(leading_dims + (slice_rows, column_count))


def general(
    hidden, norm_gain, base_weight, delta_codes, delta_scales, delta_zeros, variant_ids, positions
):
    row_count, half_width = hidden.shape
    device_count = lax.axis_size("variant")
    variant_count = device_count // OWNERS
    capacity = min(row_count, max(2, 2 * row_count // variant_count))
    slice_rows = delta_codes.shape[2]
    column_count = base_weight.shape[1]
    floats = hidden.astype(jnp.float32)
    local_squares = jnp.sum(floats * floats, axis=1)
    all_squares = lax.psum(local_squares, "tensor")
    full_width = half_width * lax.axis_size("tensor")
    normed = (
        floats
        * lax.rsqrt(all_squares / full_width + epsilon)[:, None]
        * norm_gain.astype(jnp.float32)[None, :]
    ).astype(jnp.bfloat16)
    chosen = variant_ids[:, 0]
    labels = jnp.arange(variant_count, dtype=jnp.int32)
    member = (chosen[:, None] == labels[None, :]).astype(jnp.int32)
    earlier = jnp.cumsum(member, axis=0) - member
    ranking = jnp.sum(earlier * member, axis=1)
    target_slot = chosen * capacity + ranking
    slot_labels = jnp.arange(variant_count * capacity, dtype=jnp.int32)
    placing = slot_labels[:, None] == target_slot[None, :]
    place_send = placing.astype(jnp.bfloat16).reshape(variant_count, capacity, row_count)
    place_back = placing.astype(jnp.float32)
    feature_pieces = normed.reshape(row_count, OWNERS, slice_rows)
    outgoing = jnp.einsum(
        "vcr,rjs->vjcs", place_send, feature_pieces, preferred_element_type=jnp.float32
    )
    outgoing = outgoing.astype(jnp.bfloat16).reshape(device_count, capacity, slice_rows)
    local_delta = dequantize(delta_codes[0, 0], delta_scales[0, 0], delta_zeros[0, 0]).astype(
        jnp.bfloat16
    )
    products = jnp.einsum(
        "acs,sk->ack",
        lax.all_to_all(outgoing, "variant", split_axis=0, concat_axis=0, tiled=True),
        local_delta,
        preferred_element_type=jnp.float32,
    )
    base_part = jnp.dot(normed, base_weight, preferred_element_type=jnp.float32)
    returned = lax.all_to_all(products, "variant", split_axis=0, concat_axis=0, tiled=True)
    summed = jnp.sum(returned.reshape(variant_count, OWNERS, capacity, column_count), axis=1)
    summed = summed.reshape(variant_count * capacity, column_count)
    delta_rows = jnp.einsum("sr,sk->rk", place_back, summed, precision=lax.Precision.HIGHEST)
    combined = lax.psum_scatter(base_part + delta_rows, "tensor", scatter_dimension=1, tiled=True)
    return rotate_keys(combined, positions)


def norm_kernel(rows_ref, gain_ref, out_ref, gains_ref, rows, gain, arrived):
    copies = [
        pltpu.make_async_copy(gain_ref, gain, arrived.at[0]),
        pltpu.make_async_copy(rows_ref, rows, arrived.at[1]),
    ]
    for copy in copies:
        copy.start()
    copies[0].wait()
    gains_ref[...] = gain[...].astype(jnp.float32).reshape(gains_ref.shape)
    copies[1].wait()
    out_ref[...] = norm_rows(rows[...], gains_ref[...])


def weight_kernel(
    core_ref,
    first_ref,
    own_codes,
    own_scales,
    own_zeros,
    base_ref,
    other_codes,
    other_scales,
    other_zeros,
    out_ref,
    codes,
    scales,
    zeros,
    base,
    arrived,
):
    slice_rows = codes.shape[0]
    core = core_ref[0]
    starts = [pl.multiple_of((1 - core) * slice_rows, slice_rows), pl.multiple_of(core * slice_rows, slice_rows)]
    first = first_ref[0] * slice_rows
    copies = [
        pltpu.make_async_copy(
            base_ref.at[pl.ds(pl.multiple_of(first + starts[0], slice_rows), slice_rows)], base.at[0], arrived.at[0]
        ),
        pltpu.make_async_copy(own_scales, scales, arrived.at[1]),
        pltpu.make_async_copy(own_zeros, zeros, arrived.at[2]),
        pltpu.make_async_copy(own_codes, codes, arrived.at[3]),
        pltpu.make_async_copy(
            base_ref.at[pl.ds(pl.multiple_of(first + starts[1], slice_rows), slice_rows)], base.at[1], arrived.at[4]
        ),
    ]
    for copy in copies:
        copy.start()
    group_count = scales.shape[0]
    size = slice_rows // group_count
    sources = [(other_codes, other_scales, other_zeros), (codes, scales, zeros)]
    for member, (member_codes, member_scales, member_zeros) in enumerate(sources):
        for copy in copies[1:] if member else copies[:1]:
            copy.wait()
        for group in range(group_count):
            rows = slice(group * size, (group + 1) * size)
            delta = member_codes[rows].astype(jnp.float32) - member_zeros[group : group + 1]
            delta = delta * member_scales[group : group + 1]
            target = pl.ds(pl.multiple_of(starts[member] + group * size, size), size)
            out_ref[target] = (base[member, rows].astype(jnp.float32) + delta).astype(jnp.bfloat16)


def norm_rows(rows, gain):
    floats = rows.astype(jnp.float32)
    mean_square = jnp.sum(floats * floats, axis=1, keepdims=True) / rows.shape[1]
    return (floats * lax.rsqrt(mean_square + epsilon) * gain).astype(jnp.bfloat16)


def pieces_kernel(orders, piece_ref, core_ref, own_ref, other_ref, gain_ref, *rest):
    outs, normed_ref = rest[:-1], rest[-1]
    row_count = own_ref.shape[0]
    core = core_ref[0]
    normed_ref[pl.ds(pl.multiple_of(core * row_count, row_count), row_count)] = own_ref[...]
    other_rows = pl.ds(pl.multiple_of((1 - core) * row_count, row_count), row_count)
    normed_ref[other_rows] = norm_rows(other_ref[...], gain_ref[...])
    for index, out_ref in enumerate(outs):
        piece_width = out_ref.shape[1]
        offset = jnp.where(core == 0, orders[0][index] % len(outs), orders[1][index] % len(outs))
        start = pl.multiple_of((piece_ref[0] ^ offset) * piece_width, piece_width)
        out_ref[...] = normed_ref[:, pl.ds(start, piece_width)]


def product_kernel(rows_ref, weight_ref, out_ref):
    out_ref[...] = jnp.dot(rows_ref[...], weight_ref[...], preferred_element_type=jnp.float32).astype(out_ref.dtype)


def sum_kernel(orders, core_ref, *rest):
    parts, (kept_ref, sent_ref, total_ref) = rest[:-3], rest[-3:]
    core = core_ref[0]
    for member, order in enumerate(orders):

        @pl.when(core == member)
        def _(order=order):
            for kind in range(2):
                chosen = [part for part, distance in zip(parts, order) if (distance < len(order)) == bool(kind)]
                total_ref[kind] = sum((part[...].astype(jnp.float32) for part in chosen), jnp.zeros(total_ref.shape[1:], jnp.float32))

    row_count = kept_ref.shape[1]
    kept_ref[...] = total_ref[:, pl.ds(pl.multiple_of(core * row_count, row_count), row_count)]
    sent_ref[...] = total_ref[:, pl.ds(pl.multiple_of((1 - core) * row_count, row_count), row_count)]


def finish_kernel(variant_ref, ids_ref, kept_ref, received_ref, cosine_ref, sine_ref, out_ref):
    row_count, column_count = out_ref.shape
    square = (row_count, row_count)
    diagonal = lax.broadcasted_iota(jnp.int32, square, 0) == lax.broadcasted_iota(jnp.int32, square, 1)
    ids = jnp.sum(jnp.where(diagonal, ids_ref[...], 0), axis=1, keepdims=True)
    near = ids == variant_ref[0]
    total = jnp.where(near, kept_ref[1] + received_ref[1], kept_ref[0] + received_ref[0])
    for head in range(column_count // HEAD):
        columns = slice(head * HEAD, (head + 1) * HEAD)
        block = total[:, columns]
        swapped = pltpu.roll(block, HEAD // 2, 1)
        out_ref[:, columns] = (block * cosine_ref[...] + swapped * sine_ref[...]).astype(out_ref.dtype)


def turn_factors(position):
    half_size = HEAD // 2
    frequency = rope_theta ** (-(jnp.arange(half_size, dtype=jnp.float32) * 2.0 / HEAD))
    angles = position.astype(jnp.float32)[:, None] * frequency[None, :]
    cosine, sine = jnp.cos(angles), jnp.sin(angles)
    return jnp.concatenate([cosine, cosine], axis=1), jnp.concatenate([-sine, sine], axis=1)


VMEM = pl.BlockSpec(memory_space=pltpu.VMEM)
SMEM = pl.BlockSpec(memory_space=pltpu.SMEM)
ANY = pl.BlockSpec(memory_space=pl.ANY)


def in_hbm(array):
    return pltpu.with_memory_space_constraint(array, pltpu.HBM)


def paired(
    hidden, norm_gain, base_weight, delta_codes, delta_scales, delta_zeros, variant_ids, positions
):
    row_count, width = hidden.shape
    device_count = lax.axis_size("variant")
    pieces = OWNERS // 2
    slice_rows, column_count = delta_codes.shape[2:]
    place = lax.axis_index("variant")
    core = lax.rem(place, 2)
    piece = lax.div(lax.rem(place, OWNERS), 2)
    variant = lax.div(place, OWNERS)
    swap = [(index, index ^ 1) for index in range(device_count)]
    orders = ((7, 5, 4, 0), (6, 3, 2, 1))
    steps = list(zip(*orders))

    crossed = (1, 0, 1, 0)

    def route(distances, cross, turned=0):
        return [(index, (index ^ (2 * distances[(index % 2) ^ turned])) ^ cross) for index in range(device_count)]

    slice_shape, group_shape = (slice_rows, column_count), delta_scales.shape[2:]
    own_codes, own_scales, own_zeros = delta_codes[0, 0], delta_scales[0, 0], delta_zeros[0, 0]
    other_hidden = lax.ppermute(hidden, "variant", swap)
    other_scales = lax.ppermute(own_scales, "variant", swap)
    other_zeros = lax.ppermute(own_zeros, "variant", swap)
    normed, gains = pl.pallas_call(
        norm_kernel,
        out_shape=[jax.ShapeDtypeStruct((row_count, width), jnp.bfloat16), jax.ShapeDtypeStruct((1, width), jnp.float32)],
        in_specs=[ANY] * 2,
        out_specs=[VMEM] * 2,
        scratch_shapes=[
            pltpu.VMEM((row_count, width), jnp.bfloat16),
            pltpu.VMEM((width,), jnp.bfloat16),
            pltpu.SemaphoreType.DMA((2,)),
        ],
        compiler_params=pltpu.CompilerParams(vmem_limit_bytes=16 << 20),
        name="norm",
    )(in_hbm(hidden), in_hbm(norm_gain))
    other_hidden, other_scales, other_zeros, codes, normed = lax.optimization_barrier(
        (other_hidden, other_scales, other_zeros, own_codes, normed)
    )
    other_codes = lax.ppermute(codes, "variant", swap)
    outgoing = pl.pallas_call(
        functools.partial(pieces_kernel, orders),
        out_shape=[jax.ShapeDtypeStruct((2 * row_count, width // pieces), jnp.bfloat16)] * len(steps),
        in_specs=[SMEM, SMEM, VMEM, VMEM, VMEM],
        out_specs=[VMEM] * len(steps),
        scratch_shapes=[pltpu.VMEM((2 * row_count, width), jnp.bfloat16)],
        compiler_params=pltpu.CompilerParams(vmem_limit_bytes=16 << 20),
        name="pieces",
    )(piece[None], core[None], normed, other_hidden, gains)
    weight = pl.pallas_call(
        weight_kernel,
        out_shape=jax.ShapeDtypeStruct((2 * slice_rows, column_count), jnp.bfloat16),
        in_specs=[SMEM, SMEM] + [ANY] * 4 + [VMEM] * 3,
        out_specs=VMEM,
        scratch_shapes=[
            pltpu.VMEM(slice_shape, jnp.bfloat16),
            pltpu.VMEM(group_shape, jnp.float32),
            pltpu.VMEM(group_shape, jnp.float32),
            pltpu.VMEM((2,) + slice_shape, jnp.bfloat16),
            pltpu.SemaphoreType.DMA((5,)),
        ],
        compiler_params=pltpu.CompilerParams(vmem_limit_bytes=16 << 20),
        name="weight",
    )(
        core[None],
        (piece * 2)[None],
        in_hbm(own_codes),
        in_hbm(own_scales),
        in_hbm(own_zeros),
        in_hbm(base_weight),
        other_codes,
        other_scales,
        other_zeros,
    )
    weight, positions = lax.optimization_barrier((weight, positions))
    incoming = [lax.ppermute(rows, "variant", route(distances, cross)) for rows, distances, cross in zip(outgoing, steps, crossed)]
    parts = [None] * len(steps)
    for step in range(len(steps)):
        product = pl.pallas_call(
            product_kernel,
            out_shape=jax.ShapeDtypeStruct((2 * row_count, column_count), jnp.bfloat16),
            in_specs=[VMEM, VMEM],
            out_specs=VMEM,
            compiler_params=pltpu.CompilerParams(vmem_limit_bytes=16 << 20),
            name="product",
        )(incoming[step], weight)
        parts[step] = lax.ppermute(product, "variant", route(steps[step], 1 ^ crossed[step], crossed[step]))
    kept, sent = pl.pallas_call(
        functools.partial(sum_kernel, orders[::-1]),
        out_shape=[jax.ShapeDtypeStruct((2, row_count, column_count), jnp.float32)] * 2,
        in_specs=[SMEM] + [VMEM] * len(parts),
        out_specs=[VMEM] * 2,
        scratch_shapes=[pltpu.VMEM((2, 2 * row_count, column_count), jnp.float32)],
        compiler_params=pltpu.CompilerParams(vmem_limit_bytes=8 << 20),
        name="sum",
    )(core[None], *parts)
    received = lax.ppermute(sent, "variant", swap)
    cosine, sine = turn_factors(positions)
    return pl.pallas_call(
        finish_kernel,
        out_shape=jax.ShapeDtypeStruct((row_count, column_count), jnp.bfloat16),
        in_specs=[SMEM] + [VMEM] * 5,
        out_specs=VMEM,
        compiler_params=pltpu.CompilerParams(vmem_limit_bytes=8 << 20),
        name="finish",
    )(variant[None], variant_ids.T, kept, received, cosine, sine)


def solution(mesh):
    devices = mesh.shape["variant"]
    small = mesh.shape["tensor"] == 1 and devices == 2 * OWNERS
    per_device = paired if small else general
    in_specs = (
        P(("groups", "variant"), "tensor"),
        P("tensor"),
        P("tensor", None),
        P("tensor", ("groups", "variant"), None, None),
        P("tensor", ("groups", "variant"), None, None),
        P("tensor", ("groups", "variant"), None, None),
        P(("groups", "variant"), None),
        P(("groups", "variant")),
    )
    out_specs = P(("groups", "variant"), "tensor")
    return jax.shard_map(
        per_device, mesh=mesh, in_specs=in_specs, out_specs=out_specs, check_vma=False
    )
```
